256 devices in a mesh: dp: 8 (over z_lo, x), tok: 32 (over z_hi, y, core).
Axes of the slice: x: 4, y: 4, z: 8 (z_hi: 4, z_lo: 2; z = z_hi * 2 + z_lo), core: 2. Of those that a mesh axis runs over, the one named last changes fastest.
Arguments:
- qkv_local: bfloat16 [8, 64, 96, 3840], P('dp', 'tok'), may hold values from -4.5 to 4.5
- qkv_global: bfloat16 [8, 64, 96, 3840], P('dp', 'tok'), may hold values from -4.5 to 4.5
- positions: int32 [8, 64, 96], P('dp', 'tok'), may hold values from 0 to 191, as said below
- slopes: float32 [8], replicated, may hold values from 0.02 to 0.5
- cotangent: bfloat16 [8, 64, 96, 1280], P('dp', 'tok'), may hold values from -6 to 6
- w_out_local: bfloat16 [1280, 1280], replicated, may hold values from -0.15625 to 0.15625
- w_out_global: bfloat16 [1280, 1280], replicated, may hold values from -0.15625 to 0.15625
Outputs:
- d_qkv_local: bfloat16 [8, 64, 96, 3840], P('dp', 'tok')
- d_qkv_global: bfloat16 [8, 64, 96, 3840], P('dp', 'tok')
- grad_w_local: float32 [1280, 1280], P('tok')
- grad_w_global: float32 [1280, 1280], P('tok')
The draws below stay inside these ranges and needn't reach their ends.
Inputs may be any that keep to these rules, and one draw needn't show every extreme that they name: In every window the 96 entries are distinct and increasing positions of a window of 12 rows and 16 columns, numbered row by row.
All inputs are finite; a program needn't handle non-finite values.
Results may differ from the reference program's by a relative error of at most 0.0063.
Values may be sent and summed in bfloat16 or wider, within the bound.
No kernel may reach another device: no remote copies, remote signals or barrier semaphores. Data moves between devices by JAX's collectives and lax.ppermute only.
A program may use at most 128 MiB of HBM per device.

```python
import math
import jax
import jax.numpy as jnp
from jax import lax

D = 1280
HEADS = 8
HEAD_DIM = 160
WC = 16
HD = 1280
SAMPLES = 8
KEEP = 96
NWIN = 64


def draw_qkv_local(key, part):
    key = jax.random.fold_in(key, 11)
    first_key = jax.random.fold_in(key, 0)
    full_shape = (SAMPLES, NWIN, KEEP, 3, HEADS, HEAD_DIM)
    sampled = jax.random.normal(first_key, full_shape, jnp.float32)
    sampled = jnp.clip(sampled, -4.5, 4.5)
    return sampled.reshape(SAMPLES, NWIN, KEEP, 3 * HEADS * HEAD_DIM).astype(jnp.bfloat16)


def draw_qkv_global(key, part):
    key = jax.random.fold_in(key, 23)
    first_key = jax.random.fold_in(key, 0)
    full_shape = (SAMPLES, NWIN, KEEP, 3, HEADS, HEAD_DIM)
    sampled = jax.random.normal(first_key, full_shape, jnp.float32)
    sampled = jnp.clip(sampled, -4.5, 4.5)
    return sampled.reshape(SAMPLES, NWIN, KEEP, 3 * HEADS * HEAD_DIM).astype(jnp.bfloat16)


def draw_positions(key, part):
    key = jax.random.fold_in(key, 5)
    window_keys = jax.random.split(key, SAMPLES * NWIN)

    def one_window(window_key):
        return jax.random.permutation(window_key, 2 * KEEP)[:KEEP]
    chosen = jax.vmap(one_window)(window_keys)
    ordered = jnp.sort(chosen, axis=1)
    return ordered.reshape(SAMPLES, NWIN, KEEP).astype(jnp.int32)


def block_levels(own_key, shape, pieces, low, high):
    level = 1.0
    for dim, parts in pieces:
        draws = jax.random.uniform(jax.random.fold_in(jax.random.fold_in(own_key, 6), dim), (parts,), jnp.float32, low / len(pieces), high / len(pieces))
        level = level * jnp.repeat(jnp.exp(draws), shape[dim] // parts).reshape((-1,) + (1,) * (len(shape) - 1 - dim))
    return level


def bell_draw(key, shape, spread, reach, cuts=(), dtype=jnp.bfloat16):
    gain = block_levels(key, shape, cuts, -0.22, 0.18) if cuts else 1.0
    result = jax.random.normal(key, shape, jnp.float32) * spread * gain
    return jnp.minimum(jnp.maximum(result, -reach), reach).astype(dtype)


def setup_inputs(seed: int = 0) -> dict:
    streams_of = jax.random.split(jax.random.key(seed), 8)
    return {
        "qkv_local": draw_qkv_local(jax.random.fold_in(streams_of[7], 71), 0),
        "qkv_global": draw_qkv_global(jax.random.fold_in(streams_of[7], 71), 0),
        "positions": draw_positions(jax.random.fold_in(streams_of[7], 71), 0),
        "slopes": jnp.clip(jnp.exp(jax.random.uniform(streams_of[3], (HEADS,), jnp.float32, math.log(0.02), math.log(0.5))), 0.02, 0.5),
        "cotangent": bell_draw(streams_of[4], (SAMPLES, NWIN, KEEP, D), 1.0, 6.0, ((0, 8), (1, 32))),
        "w_out_local": bell_draw(streams_of[5], (HD, D), HD ** -0.5, 0.15625),
        "w_out_global": bell_draw(streams_of[6], (HD, D), HD ** -0.5, 0.15625),
    }


HIGHEST_PRECISION = lax.Precision.HIGHEST


def widen(tensor):
    return tensor.astype(jnp.float32)


def attention_back(queries, key_block, values, grad_out, distance_bias):
    scaling = queries.shape[-1] ** -0.5
    scores = jnp.einsum("bhid,bhjd->bhij", widen(queries), widen(key_block), precision=HIGHEST_PRECISION) * scaling + distance_bias
    row_top = jnp.max(scores, axis=-1, keepdims=True)
    weights = jnp.exp(scores - row_top)
    probs_full = weights / jnp.sum(weights, axis=-1, keepdims=True)
    probs_low = widen(lax.optimization_barrier(probs_full.astype(jnp.bfloat16)))
    mixture = jnp.einsum("bhij,bhjd->bhid", probs_low, widen(values), precision=HIGHEST_PRECISION).astype(jnp.bfloat16)
    grad_probs = jnp.einsum("bhid,bhjd->bhij", widen(grad_out), widen(values), precision=HIGHEST_PRECISION)
    inner_sum = jnp.sum(probs_full * grad_probs, axis=-1, keepdims=True)
    grad_scores = widen(lax.optimization_barrier((probs_full * (grad_probs - inner_sum)).astype(jnp.bfloat16)))
    grad_queries = (jnp.einsum("bhij,bhjd->bhid", grad_scores, widen(key_block), precision=HIGHEST_PRECISION) * scaling).astype(jnp.bfloat16)
    grad_keys = (jnp.einsum("bhij,bhid->bhjd", grad_scores, widen(queries), precision=HIGHEST_PRECISION) * scaling).astype(jnp.bfloat16)
    grad_values = jnp.einsum("bhij,bhid->bhjd", probs_low, widen(grad_out), precision=HIGHEST_PRECISION).astype(jnp.bfloat16)
    return mixture, grad_queries, grad_keys, grad_values


def unpack(packed):
    shaped = packed.reshape(packed.shape[:-1] + (3, HEADS, HEAD_DIM))
    return shaped[..., 0, :, :], shaped[..., 1, :, :], shaped[..., 2, :, :]


def one_sample(inputs):
    qkv_local, qkv_global, positions, cotangent, slopes, w_out_local, w_out_global = inputs
    flat_grad = cotangent.reshape(NWIN * KEEP, D)
    pos_rows = positions // WC
    pos_cols = positions % WC
    distance = (jnp.abs(pos_rows[:, :, None] - pos_rows[:, None, :]) + jnp.abs(pos_cols[:, :, None] - pos_cols[:, None, :])).astype(jnp.float32)
    distance_bias = -(slopes[None, :, None, None] * distance[:, None, :, :])

    grad_local = jnp.dot(flat_grad, w_out_local.T, preferred_element_type=jnp.float32).astype(jnp.bfloat16)
    grad_local = grad_local.reshape(NWIN, KEEP, HEADS, HEAD_DIM)
    queries, key_block, values = unpack(qkv_local)

    def to_heads(tensor):
        return jnp.transpose(tensor, (0, 2, 1, 3))

    mixture, grad_queries, grad_keys, grad_values = attention_back(to_heads(queries), to_heads(key_block), to_heads(values), to_heads(grad_local), distance_bias)
    d_local = jnp.stack([to_heads(grad_queries), to_heads(grad_keys), to_heads(grad_values)], axis=2).reshape(NWIN, KEEP, 3 * HEADS * HEAD_DIM)
    act_local = to_heads(mixture).reshape(NWIN * KEEP, HEADS * HEAD_DIM)
    term_local = jnp.dot(act_local.T, flat_grad, preferred_element_type=jnp.float32)

    grad_global = jnp.dot(flat_grad, w_out_global.T, preferred_element_type=jnp.float32).astype(jnp.bfloat16)
    grad_global = grad_global.reshape(NWIN, KEEP, HEADS, HEAD_DIM)
    queries, key_block, values = unpack(qkv_global)

    def to_groups(tensor):
        return jnp.transpose(tensor, (1, 2, 0, 3))

    def from_groups(tensor):
        return jnp.transpose(tensor, (2, 0, 1, 3))

    mixture, grad_queries, grad_keys, grad_values = attention_back(to_groups(queries), to_groups(key_block), to_groups(values), to_groups(grad_global), 0.0)
    d_global = jnp.stack([from_groups(grad_queries), from_groups(grad_keys), from_groups(grad_values)], axis=2).reshape(NWIN, KEEP, 3 * HEADS * HEAD_DIM)
    act_global = from_groups(mixture).reshape(NWIN * KEEP, HEADS * HEAD_DIM)
    term_global = jnp.dot(act_global.T, flat_grad, preferred_element_type=jnp.float32)
    return d_local, d_global, term_local, term_global


def reference(qkv_local, qkv_global, positions, slopes, cotangent, w_out_local, w_out_global):
    def per_sample(inputs):
        return one_sample(inputs + (slopes, w_out_local, w_out_global))

    d_local, d_global, terms_local, terms_global = lax.map(per_sample, (qkv_local, qkv_global, positions, cotangent))
    grad_scale = (SAMPLES * NWIN * KEEP) ** -0.5
    grad_w_local = jnp.sum(terms_local, axis=0) * grad_scale
    grad_w_global = jnp.sum(terms_global, axis=0) * grad_scale
    return d_local, d_global, grad_w_local, grad_w_global
```

```python
import functools

import jax
import jax.numpy as jnp
import numpy as np
from jax import lax
from jax.experimental import pallas as pl
from jax.experimental.pallas import tpu as pltpu
from jax.sharding import PartitionSpec as P

WC = 16
HW = 160
VMEM_LIMIT = 56 * 1024 * 1024
BF16 = jnp.bfloat16
F32 = jnp.float32


def dot_nn(a, b):
    return lax.dot_general(a, b, (((1,), (0,)), ((), ())), preferred_element_type=F32)


def dot_nt(a, b):
    return lax.dot_general(a, b, (((1,), (1,)), ((), ())), preferred_element_type=F32)


def dot_tn(a, b):
    return lax.dot_general(a, b, (((0,), (0,)), ((), ())), preferred_element_type=F32)


def order_matrix(old, new):
    sizes = dict(old)
    count = int(np.prod(list(sizes.values())))
    index = np.arange(count).reshape([s for _, s in old])
    names = [n for n, _ in old]
    moved = np.transpose(index, [names.index(n) for n in new]).reshape(-1)
    hot = np.zeros((count, count), np.float32)
    hot[np.arange(count), moved] = 1.0
    return hot


HOME = order_matrix([("s", 4), ("w", 2), ("p", 16), ("t", 3)], ["p", "s", "w", "t"])
GROUP = order_matrix([("p", 16), ("s", 4), ("w", 2), ("t", 3)], ["s", "t", "p", "w"])


def call(kernel, outs, *args, smem=(), scratch=(), flops=0, name=None):
    specs = [
        pl.BlockSpec(memory_space=pltpu.SMEM if i in smem else pltpu.VMEM)
        for i in range(len(args))
    ]
    size = sum(int(np.prod(a.shape)) * a.dtype.itemsize for a in args)
    size += sum(int(np.prod(o.shape)) * o.dtype.itemsize for o in outs)
    return pl.pallas_call(
        kernel,
        out_shape=outs,
        in_specs=specs,
        out_specs=[pl.BlockSpec(memory_space=pltpu.VMEM) for _ in outs],
        scratch_shapes=scratch,
        compiler_params=pltpu.CompilerParams(vmem_limit_bytes=VMEM_LIMIT),
        cost_estimate=pl.CostEstimate(flops=flops, bytes_accessed=size, transcendentals=0),
        name=name,
    )(*args)


def sds(shape, dtype):
    return jax.ShapeDtypeStruct(shape, dtype)


def head_masks():
    lane = lax.broadcasted_iota(jnp.int32, (1, 256), 1)
    return [
        ((lane >= 32 * h) & (lane < 32 * h + HW)).astype(F32).astype(BF16) for h in range(4)
    ]


def side_by_side(parts):
    lane = lax.broadcasted_iota(jnp.int32, (1, 128), 1)
    tiles = [parts[0][:, :128]]
    for h in range(3):
        tiles.append(jnp.where(lane < 32 * (h + 1), parts[h][:, 128:], parts[h + 1][:, :128]))
    tiles.append(parts[3][:, 128:])
    return jnp.concatenate(tiles, axis=1)


def four_heads(q, k, v, g, masks, bias=None):
    scaling = HW ** (-0.5)
    act, dq, dk, dv = [], [], [], []
    for h in range(4):
        win = slice(128 * h, 128 * h + 256)
        qh, kh, vh, gh = q[:, win], k[:, win], v[:, win], g[:, win]
        scores = dot_nt(qh * masks[h], kh) * scaling
        if bias is not None:
            scores = scores + bias(h)
        weights = jnp.exp(scores - jnp.max(scores, axis=-1, keepdims=True))
        probs = weights / jnp.sum(weights, axis=-1, keepdims=True)
        low = probs.astype(BF16)
        grad_probs = dot_nt(gh * masks[h], vh)
        inner = jnp.sum(probs * grad_probs, axis=-1, keepdims=True)
        grad_scores = (probs * (grad_probs - inner)).astype(BF16)
        act.append(dot_nn(low, vh))
        dq.append(dot_nn(grad_scores, kh) * scaling)
        dk.append(dot_tn(grad_scores, qh) * scaling)
        dv.append(dot_tn(low, gh))
    return [side_by_side(x).astype(BF16) for x in (act, dq, dk, dv)]


def row_order(place):
    x, zh, y, c = place[0], place[1], place[2], place[3]
    col = lax.broadcasted_iota(jnp.int32, (8, 1280), 1)
    half = jnp.where(col >= 640, 1, 0)
    rem = col - 640 * half

    def digit(value, size):
        total = jnp.zeros_like(value)
        for k in range(1, 4):
            total = total + jnp.where(value >= k * size, 1, 0)
        return total, value - total * size

    dx, rem = digit(rem, 160)
    dy, rem = digit(rem, 40)
    dz, rem = digit(rem, 10)
    core = (c + half) & 1
    lane = ((((zh + dz) & 3) * 4 + ((y + dy) & 3)) * 2 + core) * 40 + ((x + dx) & 3) * 10 + rem
    return lane


def in_row_order(act, place):
    lane = row_order(place)[:1]
    pieces = []
    for part in range(5):
        rows = lax.broadcasted_iota(jnp.int32, (1280, 256), 0)
        hot = (rows == lane[:, 256 * part : 256 * part + 256]).astype(F32).astype(BF16)
        pieces.append(dot_nn(act, hot).astype(BF16))
    return jnp.concatenate(pieces, axis=1)


def pack_kernel(qkv, cot, order, out):
    hot = order[...]
    for c in range(2):
        rows = slice(48 * c, 48 * c + 48)
        pieces = [qkv[w, rows, 1280 * s : 1280 * s + 1280] for s in range(3) for w in range(2)]
        pieces += [cot[w, rows, :] for w in range(2)]
        whole = jnp.concatenate(pieces, axis=0)
        out[384 * c : 384 * c + 384, :] = dot_nn(hot, whole).astype(BF16)


def unpack_kernel(got, order, out):
    hot = order[...]
    for c in range(2):
        rows = dot_tn(hot, got[384 * c : 384 * c + 384, :]).astype(BF16)
        for s in range(4):
            width = 1024 if s < 3 else 768
            for w in range(2):
                start = 96 * s + 48 * w
                out[w, 48 * c : 48 * c + 48, 1024 * s : 1024 * s + width] = rows[
                    start : start + 48, :width
                ]


def local_kernel(place, slopes, qkv, cot, weight, positions, d_out, act_own, act_other, act_all):
    masks = head_masks()
    flat = jnp.concatenate([cot[0], cot[1]], axis=0)
    g = dot_nt(flat, weight[...]).astype(BF16)
    for w in range(2):
        spread = jnp.broadcast_to(positions[w : w + 1, :], (96, 96))
        spread_t = spread.astype(F32).T.astype(jnp.int32)
        distance = (
            jnp.abs((spread >> 4) - (spread_t >> 4)) + jnp.abs((spread & 15) - (spread_t & 15))
        ).astype(F32)
        for half in range(2):
            lanes = slice(640 * half, 640 * half + 640)
            q, k, v = [
                qkv[w, :, 1280 * s + 640 * half : 1280 * s + 640 * half + 640] for s in range(3)
            ]
            act, dq, dk, dv = four_heads(
                q,
                k,
                v,
                g[96 * w : 96 * w + 96, lanes],
                masks,
                lambda h: -(slopes[4 * half + h] * distance),
            )
            act_all[96 * w : 96 * w + 96, lanes] = act
            for s, part in enumerate((dq, dk, dv)):
                d_out[w, :, 1280 * s + 640 * half : 1280 * s + 640 * half + 640] = part
    ordered = in_row_order(act_all[...], place)
    act_own[...] = ordered[:, :640]
    act_other[...] = ordered[:, 640:]


def global_kernel(place, got, weight, order, back, act_own, act_other, cot, data, grads, act_all):
    masks = head_masks()
    hot = order[...]
    for c in range(2):
        rows = dot_nn(hot, got[384 * c : 384 * c + 384, :]).astype(BF16)
        for s in range(4):
            for t in range(3):
                start = 96 * s + 32 * t
                piece = rows[start : start + 32, :]
                if s < 3:
                    data[s, 64 * t + 32 * c : 64 * t + 32 * c + 32, :] = piece
                else:
                    cot[64 * t + 32 * c : 64 * t + 32 * c + 32, :] = piece
    g = dot_nt(cot[...], weight[...]).astype(BF16)
    grads[:, 3840:] = jnp.zeros((192, 256), BF16)
    for t in range(3):
        rows = slice(64 * t, 64 * t + 64)
        for half in range(2):
            lanes = slice(640 * half, 640 * half + 640)
            q, k, v = [data[s, rows, lanes] for s in range(3)]
            act, dq, dk, dv = four_heads(q, k, v, g[rows, lanes], masks)
            act_all[rows, lanes] = act
            for s, part in enumerate((dq, dk, dv)):
                grads[rows, 1280 * s + 640 * half : 1280 * s + 640 * half + 640] = part
    for c in range(2):
        pieces = [
            grads[64 * t + 32 * c : 64 * t + 32 * c + 32, 1024 * s : 1024 * s + 1024]
            for s in range(4)
            for t in range(3)
        ]
        whole = jnp.concatenate(pieces, axis=0)
        back[384 * c : 384 * c + 384, :] = dot_tn(hot, whole).astype(BF16)
    ordered = in_row_order(act_all[...], place)
    act_own[...] = ordered[:, :640]
    act_other[...] = ordered[:, 640:]


def weight_kernel(act, act_far, cot, cot_far, own, one, two, three):
    a, b = act[...], act_far[...]
    for part in range(5):
        cols = slice(256 * part, 256 * part + 256)
        total = dot_tn(a, cot[:, cols]) + dot_tn(b, cot_far[:, cols])
        own[:, cols] = total[:160]
        for d, ref in ((1, one), (2, two), (3, three)):
            ref[:, cols] = total[160 * d : 160 * d + 160].astype(BF16)


def sum_x_kernel(own, a, b, c, kept, one, two, three):
    total = own[...] + a[...].astype(F32) + b[...].astype(F32) + c[...].astype(F32)
    kept[...] = total[:40]
    for d, ref in ((1, one), (2, two), (3, three)):
        ref[...] = total[40 * d : 40 * d + 40].astype(BF16)


def sum_y_kernel(own, a, b, c, total):
    total[...] = own[...] + a[...].astype(F32) + b[...].astype(F32) + c[...].astype(F32)


def join_kernel(local, own, a, b, c, kept, one, two, three):
    first = local[...]
    second = own[...] + a[...].astype(F32) + b[...].astype(F32) + c[...].astype(F32)
    for d, ref in ((0, kept), (1, one), (2, two), (3, three)):
        rows = slice(10 * d, 10 * d + 10)
        both = jnp.concatenate([first[rows], second[rows], jnp.zeros((4, 1280), F32)], axis=0)
        ref[...] = both.astype(ref.dtype)


def sum_z_kernel(own, a, b, c, total):
    total[...] = own[...] + a[...].astype(F32) + b[...].astype(F32) + c[...].astype(F32)


def final_kernel(scale, place, *refs):
    pieces, (local, glob) = refs[:8], refs[8:]
    x = place[0]
    sums = [(pieces[2 * d][...] + pieces[2 * d + 1][...]) * scale for d in range(4)]
    for p in range(4):
        d = (x - p) & 3
        chosen = jnp.where(
            d == 0, sums[0], jnp.where(d == 1, sums[1], jnp.where(d == 2, sums[2], sums[3]))
        )
        local[10 * p : 10 * p + 10, :] = chosen[:10]
        glob[10 * p : 10 * p + 10, :] = chosen[10:20]


def chip(z, y, c):
    return z * 8 + y * 2 + c


def swap_cores(a):
    return lax.ppermute(a, "tok", [(i, i ^ 1) for i in range(32)])


def along_x(a, d, flip=0):
    pairs = [
        (z * 4 + x, (z ^ flip) * 4 + (x + d) % 4) for z in range(2) for x in range(4)
    ]
    return lax.ppermute(a, "dp", pairs)


def along_tok(a, dz, dy):
    pairs = [
        (chip(z, y, c), chip((z + dz) % 4, (y + dy) % 4, c))
        for z in range(4)
        for y in range(4)
        for c in range(2)
    ]
    return lax.ppermute(a, "tok", pairs)


TOK_ORDER = [[chip(0, 0, c) + 2 * p for c in range(2) for p in range(16)]]


def exchange(a):
    return lax.all_to_all(
        a, "tok", split_axis=0, concat_axis=0, axis_index_groups=TOK_ORDER, tiled=True
    )


def weight_sums(act_own, act_other, cot, name):
    act_far = swap_cores(act_other)
    cot_far = swap_cores(cot)
    own, one, two, three = call(
        weight_kernel,
        [sds((160, 1280), F32)] + [sds((160, 1280), BF16)] * 3,
        act_own,
        act_far,
        cot,
        cot_far,
        flops=2 * 640 * 384 * 1280,
        name=name + "_weight",
    )
    a, b, c = along_x(one, 1), along_x(two, 2), along_x(three, 3)
    own, one, two, three = call(
        sum_x_kernel,
        [sds((40, 1280), F32)] + [sds((40, 1280), BF16)] * 3,
        own,
        a,
        b,
        c,
        name=name + "_sum_x",
    )
    return own, along_tok(one, 0, 1), along_tok(two, 0, 2), along_tok(three, 0, 3)


def per_device(qkv_local, qkv_global, positions, slopes, cotangent, w_out_local, w_out_global):
    tokens = 192 * 256
    scale = float(tokens) ** (-0.5)
    dp, tok = lax.axis_index("dp"), lax.axis_index("tok")
    place = jnp.stack([dp % 4, tok // 8, (tok // 2) % 4, tok % 2]).astype(jnp.int32)
    qkv_local = qkv_local.reshape(2, 96, 3840)
    qkv_global = qkv_global.reshape(2, 96, 3840)
    cotangent = cotangent.reshape(2, 96, 1280)
    positions = positions.reshape(2, 96)
    home = jnp.asarray(HOME, BF16)
    group = jnp.asarray(GROUP, BF16)

    (packed,) = call(
        pack_kernel, [sds((768, 1280), BF16)], qkv_global, cotangent, home, name="pack"
    )
    got = exchange(packed)

    d_local, act_own, act_other = call(
        local_kernel,
        [sds((2, 96, 3840), BF16), sds((192, 640), BF16), sds((192, 640), BF16)],
        place,
        slopes,
        qkv_local,
        cotangent,
        w_out_local,
        positions,
        smem=(0, 1),
        scratch=[pltpu.VMEM((192, 1280), BF16)],
        flops=2 * 10**9,
        name="local",
    )
    own, a, b, c = weight_sums(act_own, act_other, cotangent.reshape(192, 1280), "local")
    (sum_local,) = call(sum_y_kernel, [sds((40, 1280), F32)], own, a, b, c, name="local_sum_y")

    back, act_own, act_other, cot = call(
        global_kernel,
        [
            sds((768, 1024), BF16),
            sds((192, 640), BF16),
            sds((192, 640), BF16),
            sds((192, 1280), BF16),
        ],
        place,
        got,
        w_out_global,
        group,
        smem=(0,),
        scratch=[
            pltpu.VMEM((3, 192, 1280), BF16),
            pltpu.VMEM((192, 4096), BF16),
            pltpu.VMEM((192, 1280), BF16),
        ],
        flops=2 * 10**9,
        name="global",
    )
    returned = exchange(back)
    own, a, b, c = weight_sums(act_own, act_other, cot, "global")
    own, one, two, three = call(
        join_kernel,
        [sds((24, 1280), F32)] + [sds((24, 1280), BF16)] * 3,
        sum_local,
        own,
        a,
        b,
        c,
        name="join",
    )
    a, b, c = along_tok(one, 1, 0), along_tok(two, 2, 0), along_tok(three, 3, 0)
    (mine,) = call(sum_z_kernel, [sds((24, 1280), F32)], own, a, b, c, name="sum_z")
    pieces = [
        mine if d == 0 and flip == 0 else along_x(mine, d, flip)
        for d in range(4)
        for flip in range(2)
    ]
    grad_local, grad_global = call(
        functools.partial(final_kernel, scale),
        [sds((40, 1280), F32), sds((40, 1280), F32)],
        place,
        *pieces,
        smem=(0,),
        name="final",
    )
    (d_global,) = call(
        unpack_kernel, [sds((2, 96, 3840), BF16)], returned, home, name="unpack"
    )
    return (
        d_local.reshape(1, 2, 96, 3840),
        d_global.reshape(1, 2, 96, 3840),
        grad_local,
        grad_global,
    )


def solution(mesh):
    placed = (
        P("dp", "tok", None, None),
        P("dp", "tok", None, None),
        P("dp", "tok", None),
        P(),
        P("dp", "tok", None, None),
        P(),
        P(),
    )
    return jax.shard_map(
        per_device,
        mesh=mesh,
        in_specs=placed,
        out_specs=(
            P("dp", "tok", None, None),
            P("dp", "tok", None, None),
            P("tok", None),
            P("tok", None),
        ),
        check_vma=False,
    )
```

```python
import functools

import jax
import jax.numpy as jnp
import numpy as np
from jax import lax
from jax.experimental import pallas as pl
from jax.experimental.pallas import tpu as pltpu
from jax.sharding import PartitionSpec as P

WC = 16
HW = 160
VMEM_LIMIT = 56 * 1024 * 1024
BF16 = jnp.bfloat16
F32 = jnp.float32


def dot_nn(a, b):
    return lax.dot_general(a, b, (((1,), (0,)), ((), ())), preferred_element_type=F32)


def dot_nt(a, b):
    return lax.dot_general(a, b, (((1,), (1,)), ((), ())), preferred_element_type=F32)


def dot_tn(a, b):
    return lax.dot_general(a, b, (((0,), (0,)), ((), ())), preferred_element_type=F32)


def order_matrix(old, new):
    sizes = dict(old)
    count = int(np.prod(list(sizes.values())))
    index = np.arange(count).reshape([s for _, s in old])
    names = [n for n, _ in old]
    moved = np.transpose(index, [names.index(n) for n in new]).reshape(-1)
    hot = np.zeros((count, count), np.float32)
    hot[np.arange(count), moved] = 1.0
    return hot


HOME = order_matrix([("s", 4), ("w", 2), ("p", 16), ("t", 3)], ["p", "s", "w", "t"])
GROUP = order_matrix([("p", 16), ("s", 4), ("w", 2), ("t", 3)], ["s", "t", "p", "w"])


def call(kernel, outs, *args, smem=(), unread=(), scratch=(), flops=0, name=None):
    specs = [
        pl.BlockSpec(
            memory_space=pltpu.SMEM if i in smem else pl.ANY if i in unread else pltpu.VMEM
        )
        for i in range(len(args))
    ]
    size = sum(int(np.prod(a.shape)) * a.dtype.itemsize for a in args)
    size += sum(int(np.prod(o.shape)) * o.dtype.itemsize for o in outs)
    return pl.pallas_call(
        kernel,
        out_shape=outs,
        in_specs=specs,
        out_specs=[pl.BlockSpec(memory_space=pltpu.VMEM) for _ in outs],
        scratch_shapes=scratch,
        compiler_params=pltpu.CompilerParams(vmem_limit_bytes=VMEM_LIMIT),
        cost_estimate=pl.CostEstimate(flops=flops, bytes_accessed=size, transcendentals=0),
        name=name,
    )(*args)


def sds(shape, dtype):
    return jax.ShapeDtypeStruct(shape, dtype)


def head_masks():
    lane = lax.broadcasted_iota(jnp.int32, (1, 256), 1)
    return [
        ((lane >= 32 * h) & (lane < 32 * h + HW)).astype(F32).astype(BF16) for h in range(4)
    ]


def side_by_side(parts):
    lane = lax.broadcasted_iota(jnp.int32, (1, 128), 1)
    tiles = [parts[0][:, :128]]
    for h in range(3):
        tiles.append(jnp.where(lane < 32 * (h + 1), parts[h][:, 128:], parts[h + 1][:, :128]))
    tiles.append(parts[3][:, 128:])
    return jnp.concatenate(tiles, axis=1)


def four_heads(q, k, v, g, masks, bias=None):
    scaling = HW ** (-0.5)
    act, dq, dk, dv = [], [], [], []
    for h in range(4):
        win = slice(128 * h, 128 * h + 256)
        qh, kh, vh, gh = q[:, win], k[:, win], v[:, win], g[:, win]
        scores = dot_nt(qh * masks[h], kh) * scaling
        if bias is not None:
            scores = scores + bias(h)
        weights = jnp.exp(scores - jnp.max(scores, axis=-1, keepdims=True))
        probs = weights / jnp.sum(weights, axis=-1, keepdims=True)
        low = probs.astype(BF16)
        grad_probs = dot_nt(gh * masks[h], vh)
        inner = jnp.sum(probs * grad_probs, axis=-1, keepdims=True)
        grad_scores = (probs * (grad_probs - inner)).astype(BF16)
        act.append(dot_nn(low, vh))
        dq.append(dot_nn(grad_scores, kh) * scaling)
        dk.append(dot_tn(grad_scores, qh) * scaling)
        dv.append(dot_tn(low, gh))
    return [side_by_side(x).astype(BF16) for x in (act, dq, dk, dv)]


def row_order(place):
    x, zh, y, c = place[0], place[1], place[2], place[3]
    col = lax.broadcasted_iota(jnp.int32, (8, 1280), 1)
    half = jnp.where(col >= 640, 1, 0)
    rem = col - 640 * half

    def digit(value, size):
        total = jnp.zeros_like(value)
        for k in range(1, 4):
            total = total + jnp.where(value >= k * size, 1, 0)
        return total, value - total * size

    dx, rem = digit(rem, 160)
    dy, rem = digit(rem, 40)
    dz, rem = digit(rem, 10)
    core = (c + half) & 1
    lane = ((((zh + dz) & 3) * 4 + ((y + dy) & 3)) * 2 + core) * 40 + ((x + dx) & 3) * 10 + rem
    return lane


def in_row_order(act, place):
    lane = row_order(place)[:1]
    pieces = []
    for part in range(5):
        rows = lax.broadcasted_iota(jnp.int32, (1280, 256), 0)
        hot = (rows == lane[:, 256 * part : 256 * part + 256]).astype(F32).astype(BF16)
        pieces.append(dot_nn(act, hot).astype(BF16))
    return jnp.concatenate(pieces, axis=1)


def pack_kernel(qkv, cot, order, out):
    hot = order[...]
    for c in range(2):
        rows = slice(48 * c, 48 * c + 48)
        pieces = [qkv[w, rows, 1280 * s : 1280 * s + 1280] for s in range(3) for w in range(2)]
        pieces += [cot[w, rows, :] for w in range(2)]
        whole = jnp.concatenate(pieces, axis=0)
        out[384 * c : 384 * c + 384, :] = dot_nn(hot, whole).astype(BF16)


def unpack_kernel(got, order, out):
    hot = order[...]
    for c in range(2):
        rows = dot_tn(hot, got[384 * c : 384 * c + 384, :]).astype(BF16)
        for s in range(4):
            width = 1024 if s < 3 else 768
            for w in range(2):
                start = 96 * s + 48 * w
                out[w, 48 * c : 48 * c + 48, 1024 * s : 1024 * s + width] = rows[
                    start : start + 48, :width
                ]


def local_kernel(place, slopes, qkv, cot, weight, positions, d_out, act_own, act_other, act_all):
    masks = head_masks()
    flat = jnp.concatenate([cot[0], cot[1]], axis=0)
    g = dot_nt(flat, weight[...]).astype(BF16)
    for w in range(2):
        spread = jnp.broadcast_to(positions[w : w + 1, :], (96, 96))
        spread_t = spread.astype(F32).T.astype(jnp.int32)
        distance = (
            jnp.abs((spread >> 4) - (spread_t >> 4)) + jnp.abs((spread & 15) - (spread_t & 15))
        ).astype(F32)
        for half in range(2):
            lanes = slice(640 * half, 640 * half + 640)
            q, k, v = [
                qkv[w, :, 1280 * s + 640 * half : 1280 * s + 640 * half + 640] for s in range(3)
            ]
            act, dq, dk, dv = four_heads(
                q,
                k,
                v,
                g[96 * w : 96 * w + 96, lanes],
                masks,
                lambda h: -(slopes[4 * half + h] * distance),
            )
            act_all[96 * w : 96 * w + 96, lanes] = act
            for s, part in enumerate((dq, dk, dv)):
                d_out[w, :, 1280 * s + 640 * half : 1280 * s + 640 * half + 640] = part
    ordered = in_row_order(act_all[...], place)
    act_own[...] = ordered[:, :640]
    act_other[...] = ordered[:, 640:]


def global_kernel(place, after, got, weight, order, back, act_own, act_other, cot, data, grads, act_all):
    masks = head_masks()
    hot = order[...]
    for c in range(2):
        rows = dot_nn(hot, got[384 * c : 384 * c + 384, :]).astype(BF16)
        for s in range(4):
            for t in range(3):
                start = 96 * s + 32 * t
                piece = rows[start : start + 32, :]
                if s < 3:
                    data[s, 64 * t + 32 * c : 64 * t + 32 * c + 32, :] = piece
                else:
                    cot[64 * t + 32 * c : 64 * t + 32 * c + 32, :] = piece
    g = dot_nt(cot[...], weight[...]).astype(BF16)
    grads[:, 3840:] = jnp.zeros((192, 256), BF16)
    for t in range(3):
        rows = slice(64 * t, 64 * t + 64)
        for half in range(2):
            lanes = slice(640 * half, 640 * half + 640)
            q, k, v = [data[s, rows, lanes] for s in range(3)]
            act, dq, dk, dv = four_heads(q, k, v, g[rows, lanes], masks)
            act_all[rows, lanes] = act
            for s, part in enumerate((dq, dk, dv)):
                grads[rows, 1280 * s + 640 * half : 1280 * s + 640 * half + 640] = part
    for c in range(2):
        pieces = [
            grads[64 * t + 32 * c : 64 * t + 32 * c + 32, 1024 * s : 1024 * s + 1024]
            for s in range(4)
            for t in range(3)
        ]
        whole = jnp.concatenate(pieces, axis=0)
        back[384 * c : 384 * c + 384, :] = dot_tn(hot, whole).astype(BF16)
    ordered = in_row_order(act_all[...], place)
    act_own[...] = ordered[:, :640]
    act_other[...] = ordered[:, 640:]


def weight_kernel(act, act_far, cot, cot_far, own, one, two, three):
    a, b = act[...], act_far[...]
    for part in range(5):
        cols = slice(256 * part, 256 * part + 256)
        total = dot_tn(a, cot[:, cols]) + dot_tn(b, cot_far[:, cols])
        own[:, cols] = total[:160]
        for d, ref in ((1, one), (2, two), (3, three)):
            ref[:, cols] = total[160 * d : 160 * d + 160].astype(BF16)


def sum_x_kernel(own, a, b, c, kept, one, two, three):
    total = own[...] + a[...].astype(F32) + b[...].astype(F32) + c[...].astype(F32)
    kept[...] = total[:40]
    for d, ref in ((1, one), (2, two), (3, three)):
        ref[...] = total[40 * d : 40 * d + 40].astype(BF16)


def sum_y_kernel(own, a, b, c, total):
    total[...] = own[...] + a[...].astype(F32) + b[...].astype(F32) + c[...].astype(F32)


def join_kernel(local, own, a, b, c, kept, one, two, three):
    first = local[...]
    second = own[...] + a[...].astype(F32) + b[...].astype(F32) + c[...].astype(F32)
    for d, ref in ((0, kept), (1, one), (2, two), (3, three)):
        rows = slice(10 * d, 10 * d + 10)
        both = jnp.concatenate([first[rows], second[rows], jnp.zeros((4, 1280), F32)], axis=0)
        ref[...] = both.astype(ref.dtype)


def sum_z_kernel(own, a, b, c, total):
    one = own[...] + a[...].astype(F32) + b[...].astype(F32) + c[...].astype(F32)
    one = one.astype(BF16)
    for i in range(8):
        total[i] = one


def final_kernel(scale, pieces, local, glob):
    for x in range(4):
        both = (pieces[x].astype(F32) + pieces[4 + x].astype(F32)) * scale
        local[10 * x : 10 * x + 10, :] = both[:10]
        glob[10 * x : 10 * x + 10, :] = both[10:20]


def chip(z, y, c):
    return z * 8 + y * 2 + c


def swap_cores(a):
    return lax.ppermute(a, "tok", [(i, i ^ 1) for i in range(32)])


def along_x(a, d):
    pairs = [(z * 4 + x, z * 4 + (x + d) % 4) for z in range(2) for x in range(4)]
    return lax.ppermute(a, "dp", pairs)


def along_tok(a, dz, dy):
    pairs = [
        (chip(z, y, c), chip((z + dz) % 4, (y + dy) % 4, c))
        for z in range(4)
        for y in range(4)
        for c in range(2)
    ]
    return lax.ppermute(a, "tok", pairs)


TOK_ORDER = [[chip(0, 0, c) + 2 * p for c in range(2) for p in range(16)]]


def exchange(a):
    return lax.all_to_all(
        a, "tok", split_axis=0, concat_axis=0, axis_index_groups=TOK_ORDER, tiled=True
    )


def weight_sums(act_own, act_other, cot, name):
    act_far = swap_cores(act_other)
    cot_far = swap_cores(cot)
    own, one, two, three = call(
        weight_kernel,
        [sds((160, 1280), F32)] + [sds((160, 1280), BF16)] * 3,
        act_own,
        act_far,
        cot,
        cot_far,
        flops=2 * 640 * 384 * 1280,
        name=name + "_weight",
    )
    a, b, c = along_x(one, 1), along_x(two, 2), along_x(three, 3)
    own, one, two, three = call(
        sum_x_kernel,
        [sds((40, 1280), F32)] + [sds((40, 1280), BF16)] * 3,
        own,
        a,
        b,
        c,
        name=name + "_sum_x",
    )
    return own, one, two, three


def along_y(one, two, three):
    return along_tok(one, 0, 1), along_tok(two, 0, 2), along_tok(three, 0, 3)


def per_device(qkv_local, qkv_global, positions, slopes, cotangent, w_out_local, w_out_global):
    tokens = 192 * 256
    scale = float(tokens) ** (-0.5)
    dp, tok = lax.axis_index("dp"), lax.axis_index("tok")
    place = jnp.stack([dp % 4, tok // 8, (tok // 2) % 4, tok % 2]).astype(jnp.int32)
    qkv_local = qkv_local.reshape(2, 96, 3840)
    qkv_global = qkv_global.reshape(2, 96, 3840)
    cotangent = cotangent.reshape(2, 96, 1280)
    positions = positions.reshape(2, 96)
    home = jnp.asarray(HOME, BF16)
    group = jnp.asarray(GROUP, BF16)

    (packed,) = call(
        pack_kernel, [sds((768, 1280), BF16)], qkv_global, cotangent, home, name="pack"
    )
    got = exchange(packed)

    d_local, act_own, act_other = call(
        local_kernel,
        [sds((2, 96, 3840), BF16), sds((192, 640), BF16), sds((192, 640), BF16)],
        place,
        slopes,
        qkv_local,
        cotangent,
        w_out_local,
        positions,
        smem=(0, 1),
        scratch=[pltpu.VMEM((192, 1280), BF16)],
        flops=2 * 10**9,
        name="local",
    )
    first_own, *others = weight_sums(act_own, act_other, cotangent.reshape(192, 1280), "local")
    a, b, c = along_y(*others)
    (sum_local,) = call(
        sum_y_kernel, [sds((40, 1280), F32)], first_own, a, b, c, name="local_sum_y"
    )

    back, act_own, act_other, cot = call(
        global_kernel,
        [
            sds((768, 1024), BF16),
            sds((192, 640), BF16),
            sds((192, 640), BF16),
            sds((192, 1280), BF16),
        ],
        place,
        first_own,
        got,
        w_out_global,
        group,
        smem=(0,),
        unread=(1,),
        scratch=[
            pltpu.VMEM((3, 192, 1280), BF16),
            pltpu.VMEM((192, 4096), BF16),
            pltpu.VMEM((192, 1280), BF16),
        ],
        flops=2 * 10**9,
        name="global",
    )
    returned = exchange(back)
    own, *others = weight_sums(act_own, act_other, cot, "global")
    a, b, c = along_y(*others)
    own, one, two, three = call(
        join_kernel,
        [sds((24, 1280), F32)] + [sds((24, 1280), BF16)] * 3,
        sum_local,
        own,
        a,
        b,
        c,
        name="join",
    )
    a, b, c = along_tok(one, 1, 0), along_tok(two, 2, 0), along_tok(three, 3, 0)
    (mine,) = call(sum_z_kernel, [sds((8, 24, 1280), BF16)], own, a, b, c, name="sum_z")
    pieces = lax.all_to_all(mine, "dp", split_axis=0, concat_axis=0, tiled=True)
    grad_local, grad_global = call(
        functools.partial(final_kernel, scale),
        [sds((40, 1280), F32), sds((40, 1280), F32)],
        pieces,
        name="final",
    )
    (d_global,) = call(
        unpack_kernel, [sds((2, 96, 3840), BF16)], returned, home, name="unpack"
    )
    return (
        d_local.reshape(1, 2, 96, 3840),
        d_global.reshape(1, 2, 96, 3840),
        grad_local,
        grad_global,
    )


def solution(mesh):
    placed = (
        P("dp", "tok", None, None),
        P("dp", "tok", None, None),
        P("dp", "tok", None),
        P(),
        P("dp", "tok", None, None),
        P(),
        P(),
    )
    return jax.shard_map(
        per_device,
        mesh=mesh,
        in_specs=placed,
        out_specs=(
            P("dp", "tok", None, None),
            P("dp", "tok", None, None),
            P("tok", None),
            P("tok", None),
        ),
        check_vma=False,
    )
```

```python
import functools

import jax
import jax.numpy as jnp
import numpy as np
from jax import lax
from jax.experimental import pallas as pl
from jax.experimental.pallas import tpu as pltpu
from jax.sharding import PartitionSpec as P

WC = 16
HW = 160
VMEM_LIMIT = 56 * 1024 * 1024
BF16 = jnp.bfloat16
F32 = jnp.float32


def dot_nn(a, b):
    return lax.dot_general(a, b, (((1,), (0,)), ((), ())), preferred_element_type=F32)


def dot_nt(a, b):
    return lax.dot_general(a, b, (((1,), (1,)), ((), ())), preferred_element_type=F32)


def dot_tn(a, b):
    return lax.dot_general(a, b, (((0,), (0,)), ((), ())), preferred_element_type=F32)


def order_matrix(old, new):
    sizes = dict(old)
    count = int(np.prod(list(sizes.values())))
    index = np.arange(count).reshape([s for _, s in old])
    names = [n for n, _ in old]
    moved = np.transpose(index, [names.index(n) for n in new]).reshape(-1)
    hot = np.zeros((count, count), np.float32)
    hot[np.arange(count), moved] = 1.0
    return hot


HOME = order_matrix([("s", 4), ("w", 2), ("p", 16), ("t", 3)], ["p", "s", "w", "t"])
GROUP = order_matrix([("p", 16), ("s", 4), ("w", 2), ("t", 3)], ["s", "t", "p", "w"])


def call(kernel, outs, *args, smem=(), unread=(), scratch=(), flops=0, name=None):
    specs = [
        pl.BlockSpec(
            memory_space=pltpu.SMEM if i in smem else pl.ANY if i in unread else pltpu.VMEM
        )
        for i in range(len(args))
    ]
    size = sum(int(np.prod(a.shape)) * a.dtype.itemsize for a in args)
    size += sum(int(np.prod(o.shape)) * o.dtype.itemsize for o in outs)
    return pl.pallas_call(
        kernel,
        out_shape=outs,
        in_specs=specs,
        out_specs=[pl.BlockSpec(memory_space=pltpu.VMEM) for _ in outs],
        scratch_shapes=scratch,
        compiler_params=pltpu.CompilerParams(vmem_limit_bytes=VMEM_LIMIT),
        cost_estimate=pl.CostEstimate(flops=flops, bytes_accessed=size, transcendentals=0),
        name=name,
    )(*args)


def sds(shape, dtype):
    return jax.ShapeDtypeStruct(shape, dtype)


def head_masks():
    lane = lax.broadcasted_iota(jnp.int32, (1, 256), 1)
    return [
        ((lane >= 32 * h) & (lane < 32 * h + HW)).astype(F32).astype(BF16) for h in range(4)
    ]


def side_by_side(parts):
    lane = lax.broadcasted_iota(jnp.int32, (1, 128), 1)
    tiles = [parts[0][:, :128]]
    for h in range(3):
        tiles.append(jnp.where(lane < 32 * (h + 1), parts[h][:, 128:], parts[h + 1][:, :128]))
    tiles.append(parts[3][:, 128:])
    return jnp.concatenate(tiles, axis=1)


def four_heads(q, k, v, g, masks, bias=None):
    scaling = HW ** (-0.5)
    act, dq, dk, dv = [], [], [], []
    for h in range(4):
        win = slice(128 * h, 128 * h + 256)
        qh, kh, vh, gh = q[:, win], k[:, win], v[:, win], g[:, win]
        scores = dot_nt(qh * masks[h], kh) * scaling
        if bias is not None:
            scores = scores + bias(h)
        weights = jnp.exp(scores - jnp.max(scores, axis=-1, keepdims=True))
        probs = weights / jnp.sum(weights, axis=-1, keepdims=True)
        low = probs.astype(BF16)
        grad_probs = dot_nt(gh * masks[h], vh)
        inner = jnp.sum(probs * grad_probs, axis=-1, keepdims=True)
        grad_scores = (probs * (grad_probs - inner)).astype(BF16)
        act.append(dot_nn(low, vh))
        dq.append(dot_nn(grad_scores, kh) * scaling)
        dk.append(dot_tn(grad_scores, qh) * scaling)
        dv.append(dot_tn(low, gh))
    return [side_by_side(x).astype(BF16) for x in (act, dq, dk, dv)]


def row_order(place):
    x, zh, y, c = place[0], place[1], place[2], place[3]
    col = lax.broadcasted_iota(jnp.int32, (8, 1280), 1)
    half = jnp.where(col >= 640, 1, 0)
    rem = col - 640 * half

    def digit(value, size):
        total = jnp.zeros_like(value)
        for k in range(1, 4):
            total = total + jnp.where(value >= k * size, 1, 0)
        return total, value - total * size

    dx, rem = digit(rem, 160)
    dy, rem = digit(rem, 40)
    dz, rem = digit(rem, 10)
    core = (c + half) & 1
    lane = ((((zh + dz) & 3) * 4 + ((y + dy) & 3)) * 2 + core) * 40 + ((x + dx) & 3) * 10 + rem
    return lane


def in_row_order(act, place):
    lane = row_order(place)[:1]
    pieces = []
    for part in range(5):
        rows = lax.broadcasted_iota(jnp.int32, (1280, 256), 0)
        hot = (rows == lane[:, 256 * part : 256 * part + 256]).astype(F32).astype(BF16)
        pieces.append(dot_nn(act, hot).astype(BF16))
    return jnp.concatenate(pieces, axis=1)


def pack_kernel(qkv, cot, order, out):
    hot = order[...]
    for c in range(2):
        rows = slice(48 * c, 48 * c + 48)
        pieces = [qkv[w, rows, 1280 * s : 1280 * s + 1280] for s in range(3) for w in range(2)]
        pieces += [cot[w, rows, :] for w in range(2)]
        whole = jnp.concatenate(pieces, axis=0)
        out[384 * c : 384 * c + 384, :] = dot_nn(hot, whole).astype(BF16)


def unpack_kernel(got, order, out):
    hot = order[...]
    for c in range(2):
        rows = dot_tn(hot, got[384 * c : 384 * c + 384, :]).astype(BF16)
        for s in range(4):
            width = 1024 if s < 3 else 768
            for w in range(2):
                start = 96 * s + 48 * w
                out[w, 48 * c : 48 * c + 48, 1024 * s : 1024 * s + width] = rows[
                    start : start + 48, :width
                ]


def local_kernel(place, slopes, qkv, cot, weight, positions, d_out, act_own, act_other, act_all):
    masks = head_masks()
    flat = jnp.concatenate([cot[0], cot[1]], axis=0)
    g = dot_nt(flat, weight[...]).astype(BF16)
    for w in range(2):
        spread = jnp.broadcast_to(positions[w : w + 1, :], (96, 96))
        spread_t = spread.astype(F32).T.astype(jnp.int32)
        distance = (
            jnp.abs((spread >> 4) - (spread_t >> 4)) + jnp.abs((spread & 15) - (spread_t & 15))
        ).astype(F32)
        for half in range(2):
            lanes = slice(640 * half, 640 * half + 640)
            q, k, v = [
                qkv[w, :, 1280 * s + 640 * half : 1280 * s + 640 * half + 640] for s in range(3)
            ]
            act, dq, dk, dv = four_heads(
                q,
                k,
                v,
                g[96 * w : 96 * w + 96, lanes],
                masks,
                lambda h: -(slopes[4 * half + h] * distance),
            )
            act_all[96 * w : 96 * w + 96, lanes] = act
            for s, part in enumerate((dq, dk, dv)):
                d_out[w, :, 1280 * s + 640 * half : 1280 * s + 640 * half + 640] = part
    ordered = in_row_order(act_all[...], place)
    act_own[...] = ordered[:, :640]
    act_other[...] = ordered[:, 640:]


def global_kernel(place, after, got, weight, order, back, act_own, act_other, cot, data, grads, act_all):
    masks = head_masks()
    hot = order[...]
    for c in range(2):
        rows = dot_nn(hot, got[384 * c : 384 * c + 384, :]).astype(BF16)
        for s in range(4):
            for t in range(3):
                start = 96 * s + 32 * t
                piece = rows[start : start + 32, :]
                if s < 3:
                    data[s, 64 * t + 32 * c : 64 * t + 32 * c + 32, :] = piece
                else:
                    cot[64 * t + 32 * c : 64 * t + 32 * c + 32, :] = piece
    g = dot_nt(cot[...], weight[...]).astype(BF16)
    grads[:, 3840:] = jnp.zeros((192, 256), BF16)
    for t in range(3):
        rows = slice(64 * t, 64 * t + 64)
        for half in range(2):
            lanes = slice(640 * half, 640 * half + 640)
            q, k, v = [data[s, rows, lanes] for s in range(3)]
            act, dq, dk, dv = four_heads(q, k, v, g[rows, lanes], masks)
            act_all[rows, lanes] = act
            for s, part in enumerate((dq, dk, dv)):
                grads[rows, 1280 * s + 640 * half : 1280 * s + 640 * half + 640] = part
    for c in range(2):
        pieces = [
            grads[64 * t + 32 * c : 64 * t + 32 * c + 32, 1024 * s : 1024 * s + 1024]
            for s in range(4)
            for t in range(3)
        ]
        whole = jnp.concatenate(pieces, axis=0)
        back[384 * c : 384 * c + 384, :] = dot_tn(hot, whole).astype(BF16)
    ordered = in_row_order(act_all[...], place)
    act_own[...] = ordered[:, :640]
    act_other[...] = ordered[:, 640:]


def weight_kernel(act, act_far, cot, cot_far, own, one, two, three):
    a, b = act[...], act_far[...]
    for part in range(5):
        cols = slice(256 * part, 256 * part + 256)
        total = dot_tn(a, cot[:, cols]) + dot_tn(b, cot_far[:, cols])
        own[:, cols] = total[:160]
        for d, ref in ((1, one), (2, two), (3, three)):
            ref[:, cols] = total[160 * d : 160 * d + 160].astype(BF16)


def sum_x_kernel(own, a, b, c, kept, one, two, three):
    total = own[...] + a[...].astype(F32) + b[...].astype(F32) + c[...].astype(F32)
    kept[...] = total[:40]
    for d, ref in ((1, one), (2, two), (3, three)):
        ref[...] = total[40 * d : 40 * d + 40].astype(BF16)


def sum_y_kernel(own, a, b, c, total):
    total[...] = own[...] + a[...].astype(F32) + b[...].astype(F32) + c[...].astype(F32)


def join_kernel(local, own, a, b, c, kept, one, two, three):
    first = local[...]
    second = own[...] + a[...].astype(F32) + b[...].astype(F32) + c[...].astype(F32)
    for d, ref in ((0, kept), (1, one), (2, two), (3, three)):
        rows = slice(10 * d, 10 * d + 10)
        both = jnp.concatenate([first[rows], second[rows], jnp.zeros((4, 1280), F32)], axis=0)
        ref[...] = both.astype(ref.dtype)


def sum_z_kernel(after, own, a, b, c, total):
    one = own[...] + a[...].astype(F32) + b[...].astype(F32) + c[...].astype(F32)
    one = one.astype(BF16)
    for i in range(8):
        total[i] = one


def final_kernel(scale, after, pieces, local, glob):
    for x in range(4):
        both = (pieces[x].astype(F32) + pieces[4 + x].astype(F32)) * scale
        local[10 * x : 10 * x + 10, :] = both[:10]
        glob[10 * x : 10 * x + 10, :] = both[10:20]


def chip(z, y, c):
    return z * 8 + y * 2 + c


def swap_cores(a):
    return lax.ppermute(a, "tok", [(i, i ^ 1) for i in range(32)])


def along_x(a, d):
    pairs = [(z * 4 + x, z * 4 + (x + d) % 4) for z in range(2) for x in range(4)]
    return lax.ppermute(a, "dp", pairs)


def along_tok(a, dz, dy):
    pairs = [
        (chip(z, y, c), chip((z + dz) % 4, (y + dy) % 4, c))
        for z in range(4)
        for y in range(4)
        for c in range(2)
    ]
    return lax.ppermute(a, "tok", pairs)


TOK_ORDER = [[chip(0, 0, c) + 2 * p for c in range(2) for p in range(16)]]


def exchange(a):
    return lax.all_to_all(
        a, "tok", split_axis=0, concat_axis=0, axis_index_groups=TOK_ORDER, tiled=True
    )


def weight_sums(act_own, act_other, cot, name):
    act_far = swap_cores(act_other)
    cot_far = swap_cores(cot)
    own, one, two, three = call(
        weight_kernel,
        [sds((160, 1280), F32)] + [sds((160, 1280), BF16)] * 3,
        act_own,
        act_far,
        cot,
        cot_far,
        flops=2 * 640 * 384 * 1280,
        name=name + "_weight",
    )
    a, b, c = along_x(one, 1), along_x(two, 2), along_x(three, 3)
    own, one, two, three = call(
        sum_x_kernel,
        [sds((40, 1280), F32)] + [sds((40, 1280), BF16)] * 3,
        own,
        a,
        b,
        c,
        name=name + "_sum_x",
    )
    return own, one, two, three


def along_y(one, two, three):
    return along_tok(one, 0, 1), along_tok(two, 0, 2), along_tok(three, 0, 3)


def per_device(qkv_local, qkv_global, positions, slopes, cotangent, w_out_local, w_out_global):
    tokens = 192 * 256
    scale = float(tokens) ** (-0.5)
    dp, tok = lax.axis_index("dp"), lax.axis_index("tok")
    place = jnp.stack([dp % 4, tok // 8, (tok // 2) % 4, tok % 2]).astype(jnp.int32)
    qkv_local = qkv_local.reshape(2, 96, 3840)
    qkv_global = qkv_global.reshape(2, 96, 3840)
    cotangent = cotangent.reshape(2, 96, 1280)
    positions = positions.reshape(2, 96)
    home = jnp.asarray(HOME, BF16)
    group = jnp.asarray(GROUP, BF16)

    (packed,) = call(
        pack_kernel, [sds((768, 1280), BF16)], qkv_global, cotangent, home, name="pack"
    )
    got = exchange(packed)

    d_local, act_own, act_other = call(
        local_kernel,
        [sds((2, 96, 3840), BF16), sds((192, 640), BF16), sds((192, 640), BF16)],
        place,
        slopes,
        qkv_local,
        cotangent,
        w_out_local,
        positions,
        smem=(0, 1),
        scratch=[pltpu.VMEM((192, 1280), BF16)],
        flops=2 * 10**9,
        name="local",
    )
    first_own, *others = weight_sums(act_own, act_other, cotangent.reshape(192, 1280), "local")
    a, b, c = along_y(*others)
    (sum_local,) = call(
        sum_y_kernel, [sds((40, 1280), F32)], first_own, a, b, c, name="local_sum_y"
    )

    back, act_own, act_other, cot = call(
        global_kernel,
        [
            sds((768, 1024), BF16),
            sds((192, 640), BF16),
            sds((192, 640), BF16),
            sds((192, 1280), BF16),
        ],
        place,
        first_own,
        got,
        w_out_global,
        group,
        smem=(0,),
        unread=(1,),
        scratch=[
            pltpu.VMEM((3, 192, 1280), BF16),
            pltpu.VMEM((192, 4096), BF16),
            pltpu.VMEM((192, 1280), BF16),
        ],
        flops=2 * 10**9,
        name="global",
    )
    returned = exchange(back)
    own, *others = weight_sums(act_own, act_other, cot, "global")
    a, b, c = along_y(*others)
    own, one, two, three = call(
        join_kernel,
        [sds((24, 1280), F32)] + [sds((24, 1280), BF16)] * 3,
        sum_local,
        own,
        a,
        b,
        c,
        name="join",
    )
    a, b, c = along_tok(one, 1, 0), along_tok(two, 2, 0), along_tok(three, 3, 0)
    (mine,) = call(
        sum_z_kernel,
        [sds((8, 24, 1280), BF16)],
        returned,
        own,
        a,
        b,
        c,
        unread=(0,),
        name="sum_z",
    )
    pieces = lax.all_to_all(mine, "dp", split_axis=0, concat_axis=0, tiled=True)
    (d_global,) = call(
        unpack_kernel, [sds((2, 96, 3840), BF16)], returned, home, name="unpack"
    )
    grad_local, grad_global = call(
        functools.partial(final_kernel, scale),
        [sds((40, 1280), F32), sds((40, 1280), F32)],
        d_global,
        pieces,
        unread=(0,),
        name="final",
    )
    return (
        d_local.reshape(1, 2, 96, 3840),
        d_global.reshape(1, 2, 96, 3840),
        grad_local,
        grad_global,
    )


def solution(mesh):
    placed = (
        P("dp", "tok", None, None),
        P("dp", "tok", None, None),
        P("dp", "tok", None),
        P(),
        P("dp", "tok", None, None),
        P(),
        P(),
    )
    return jax.shard_map(
        per_device,
        mesh=mesh,
        in_specs=placed,
        out_specs=(
            P("dp", "tok", None, None),
            P("dp", "tok", None, None),
            P("tok", None),
            P("tok", None),
        ),
        check_vma=False,
    )
```

```python
import functools

import jax
import jax.numpy as jnp
import numpy as np
from jax import lax
from jax.experimental import pallas as pl
from jax.experimental.pallas import tpu as pltpu
from jax.sharding import PartitionSpec as P

WC = 16
HW = 160
VMEM_LIMIT = 56 * 1024 * 1024
BF16 = jnp.bfloat16
F32 = jnp.float32


def dot_nn(a, b):
    return lax.dot_general(a, b, (((1,), (0,)), ((), ())), preferred_element_type=F32)


def dot_nt(a, b):
    return lax.dot_general(a, b, (((1,), (1,)), ((), ())), preferred_element_type=F32)


def dot_tn(a, b):
    return lax.dot_general(a, b, (((0,), (0,)), ((), ())), preferred_element_type=F32)


def order_matrix(old, new):
    sizes = dict(old)
    count = int(np.prod(list(sizes.values())))
    index = np.arange(count).reshape([s for _, s in old])
    names = [n for n, _ in old]
    moved = np.transpose(index, [names.index(n) for n in new]).reshape(-1)
    hot = np.zeros((count, count), np.float32)
    hot[np.arange(count), moved] = 1.0
    return hot


HOME = order_matrix([("s", 2), ("o", 2), ("w", 2), ("p", 8), ("t", 6)], ["p", "s", "o", "w", "t"])
GROUP = order_matrix([("p", 8), ("s", 2), ("o", 2), ("w", 2), ("t", 6)], ["s", "o", "t", "p", "w"])
FAR_COT = order_matrix([("p", 16), ("o", 2), ("w", 2), ("t", 6)], ["o", "t", "p", "w"])
BACK = order_matrix([("s", 3), ("o", 2), ("t", 6), ("p", 8), ("w", 2)], ["p", "s", "o", "w", "t"])
UNPACK = order_matrix([("p", 8), ("s", 3), ("o", 2), ("w", 2), ("t", 6)], ["s", "o", "w", "p", "t"])


def call(kernel, outs, *args, smem=(), unread=(), scratch=(), flops=0, name=None):
    specs = [
        pl.BlockSpec(
            memory_space=pltpu.SMEM if i in smem else pl.ANY if i in unread else pltpu.VMEM
        )
        for i in range(len(args))
    ]
    size = sum(int(np.prod(a.shape)) * a.dtype.itemsize for a in args)
    size += sum(int(np.prod(o.shape)) * o.dtype.itemsize for o in outs)
    return pl.pallas_call(
        kernel,
        out_shape=outs,
        in_specs=specs,
        out_specs=[pl.BlockSpec(memory_space=pltpu.VMEM) for _ in outs],
        scratch_shapes=scratch,
        compiler_params=pltpu.CompilerParams(vmem_limit_bytes=VMEM_LIMIT),
        cost_estimate=pl.CostEstimate(flops=flops, bytes_accessed=size, transcendentals=0),
        name=name,
    )(*args)


def sds(shape, dtype):
    return jax.ShapeDtypeStruct(shape, dtype)


def head_masks():
    lane = lax.broadcasted_iota(jnp.int32, (1, 256), 1)
    return [
        ((lane >= 32 * h) & (lane < 32 * h + HW)).astype(F32).astype(BF16) for h in range(4)
    ]


def side_by_side(parts):
    lane = lax.broadcasted_iota(jnp.int32, (1, 128), 1)
    tiles = [parts[0][:, :128]]
    for h in range(3):
        tiles.append(jnp.where(lane < 32 * (h + 1), parts[h][:, 128:], parts[h + 1][:, :128]))
    tiles.append(parts[3][:, 128:])
    return jnp.concatenate(tiles, axis=1)


def probabilities(q, k, masks, bias=None):
    scaling = HW ** (-0.5)
    probs = []
    for h in range(4):
        win = slice(128 * h, 128 * h + 256)
        scores = dot_nt(q[:, win] * masks[h], k[:, win]) * scaling
        if bias is not None:
            scores = scores + bias(h)
        weights = jnp.exp(scores - jnp.max(scores, axis=-1, keepdims=True))
        probs.append(weights / jnp.sum(weights, axis=-1, keepdims=True))
    return probs


def mixture(probs, v):
    parts = [
        dot_nn(probs[h].astype(BF16), v[:, 128 * h : 128 * h + 256]) for h in range(4)
    ]
    return side_by_side(parts).astype(BF16)


def gradients(probs, q, k, v, g, masks):
    scaling = HW ** (-0.5)
    dq, dk, dv = [], [], []
    for h in range(4):
        win = slice(128 * h, 128 * h + 256)
        grad_probs = dot_nt(g[:, win] * masks[h], v[:, win])
        inner = jnp.sum(probs[h] * grad_probs, axis=-1, keepdims=True)
        grad_scores = (probs[h] * (grad_probs - inner)).astype(BF16)
        dq.append(dot_nn(grad_scores, k[:, win]) * scaling)
        dk.append(dot_tn(grad_scores, q[:, win]) * scaling)
        dv.append(dot_tn(probs[h].astype(BF16), g[:, win]))
    return [side_by_side(x).astype(BF16) for x in (dq, dk, dv)]


def row_order(place):
    x, zh, y = place[0], place[1], place[2]
    rem = lax.broadcasted_iota(jnp.int32, (8, 640), 1)

    def digit(value, size):
        total = jnp.zeros_like(value)
        for k in range(1, 4):
            total = total + jnp.where(value >= k * size, 1, 0)
        return total, value - total * size

    dx, rem = digit(rem, 160)
    dy, rem = digit(rem, 40)
    df, rem = digit(rem, 10)
    to = (zh + df) & 3
    return (((to >> 1) * 4 + ((y + dy) & 3)) * 2 + (to & 1)) * 40 + ((x + dx) & 3) * 10 + rem


def row_hot(place):
    lane = row_order(place)[:1]
    rows = lax.broadcasted_iota(jnp.int32, (640, 640), 0)
    return (rows == lane).astype(F32).astype(BF16)


def lanes_of(section, core):
    return pl.ds(pl.multiple_of(1280 * section + 640 * core, 128), 640)


def far_kernel(place, qkv, out):
    for s in range(3):
        for w in range(2):
            out[w, :, 640 * s : 640 * s + 640] = qkv[w, :, lanes_of(s, 1 - place[3])]


def pack_kernel(place, qkv, far, cot, order, out):
    hot = order[...]
    for group in range(2):
        rows = slice(48 * group, 48 * group + 48)

        def section(s):
            own = [qkv[w, rows, lanes_of(s, place[3])] for w in range(2)]
            return own + [far[w, rows, 640 * s : 640 * s + 640] for w in range(2)]

        cots = [cot[w, rows, 640 * half : 640 * half + 640] for half in range(2) for w in range(2)]
        for part, pieces in enumerate((section(0) + section(1), section(2) + cots)):
            sent = dot_nn(hot, jnp.concatenate(pieces, axis=0)).astype(BF16)
            for p in range(8):
                start = 96 * (8 * group + p) + 48 * part
                out[start : start + 48, :] = sent[48 * p : 48 * p + 48, :]


def unpack_kernel(got, order, mine, other):
    hot = order[...]
    for group in range(2):
        rows = dot_nn(hot, got[576 * group : 576 * group + 576, :]).astype(BF16)
        for s in range(3):
            for o, ref in enumerate((mine, other)):
                for w in range(2):
                    start = 48 * ((s * 2 + o) * 2 + w)
                    ref[w, 48 * group : 48 * group + 48, 640 * s : 640 * s + 640] = rows[
                        start : start + 48, :
                    ]


def merge_kernel(place, mine, far, out):
    for s in range(3):
        for w in range(2):
            out[w, :, lanes_of(s, place[3])] = mine[w, :, 640 * s : 640 * s + 640]
            out[w, :, lanes_of(s, 1 - place[3])] = far[w, :, 640 * s : 640 * s + 640]


def local_kernel(place, slopes, qkv, cot, weight, positions, d_out, act_own, act_other, act_all):
    masks = head_masks()
    flat = jnp.concatenate([cot[0], cot[1]], axis=0)
    g = dot_nt(flat, weight[...]).astype(BF16)
    for w in range(2):
        spread = jnp.broadcast_to(positions[w : w + 1, :], (96, 96))
        spread_t = spread.astype(F32).T.astype(jnp.int32)
        distance = (
            jnp.abs((spread >> 4) - (spread_t >> 4)) + jnp.abs((spread & 15) - (spread_t & 15))
        ).astype(F32)
        for half in range(2):
            lanes = slice(640 * half, 640 * half + 640)
            q, k, v = [
                qkv[w, :, 1280 * s + 640 * half : 1280 * s + 640 * half + 640] for s in range(3)
            ]
            probs = probabilities(q, k, masks, lambda h: -(slopes[4 * half + h] * distance))
            act_all[96 * w : 96 * w + 96, lanes] = mixture(probs, v)
            grads = gradients(probs, q, k, v, g[96 * w : 96 * w + 96, lanes], masks)
            for s, part in enumerate(grads):
                d_out[w, :, 1280 * s + 640 * half : 1280 * s + 640 * half + 640] = part
    hot = row_hot(place)
    act_own[...] = dot_nn(act_all[:, lanes_of(0, place[3])], hot).astype(BF16)
    act_other[...] = dot_nn(act_all[:, lanes_of(0, 1 - place[3])], hot).astype(BF16)


def group_kernel(place, after, got, order, data, cot, probs_out, act, act_all):
    masks = head_masks()
    hot = order[...]
    for group in range(2):
        for part in range(2):
            pieces = [
                got[96 * (8 * group + p) + 48 * part : 96 * (8 * group + p) + 48 * part + 48, :]
                for p in range(8)
            ]
            rows = dot_nn(hot, jnp.concatenate(pieces, axis=0)).astype(BF16)
            for s in range(2):
                for o in range(2):
                    for t in range(6):
                        start = 16 * ((s * 2 + o) * 6 + t)
                        piece = rows[start : start + 16, :]
                        to = slice(32 * t + 16 * group, 32 * t + 16 * group + 16)
                        if part == 1 and s == 1:
                            cot[to, 640 * o : 640 * o + 640] = piece
                        else:
                            data[2 * part + s, o, to, :] = piece
    for t in range(6):
        rows = slice(32 * t, 32 * t + 32)
        q, k, v = [
            jnp.concatenate([data[s, 0, rows, :], data[s, 1, rows, :]], axis=0) for s in range(3)
        ]
        probs = probabilities(q, k, masks)
        for h in range(4):
            probs_out[4 * t + h] = probs[h]
        mixed = mixture(probs, v)
        act_all[32 * t : 32 * t + 32, :] = mixed[:32]
        act_all[192 + 32 * t : 192 + 32 * t + 32, :] = mixed[32:]
    act[...] = dot_nn(act_all[...], row_hot(place)).astype(BF16)


def group_back_kernel(place, probs_in, data, cot, cot_far, weight, order, back, grads):
    masks = head_masks()
    hot = order[...]
    own_rows = weight[pl.ds(pl.multiple_of(640 * place[3], 128), 640), :]
    g_own = dot_nt(cot[...], own_rows).astype(BF16)
    g_far = dot_nt(cot_far[...], own_rows).astype(BF16)
    for t in range(6):
        rows = slice(32 * t, 32 * t + 32)
        q, k, v = [
            jnp.concatenate([data[s, 0, rows, :], data[s, 1, rows, :]], axis=0) for s in range(3)
        ]
        g = jnp.concatenate([g_own[rows], g_far[rows]], axis=0)
        probs = [probs_in[4 * t + h] for h in range(4)]
        for s, part in enumerate(gradients(probs, q, k, v, g, masks)):
            grads[s, 0, rows, :] = part[:32]
            grads[s, 1, rows, :] = part[32:]
    for group in range(2):
        pieces = [
            grads[s, o, 32 * t + 16 * group : 32 * t + 16 * group + 16, :]
            for s in range(3)
            for o in range(2)
            for t in range(6)
        ]
        whole = jnp.concatenate(pieces, axis=0)
        back[576 * group : 576 * group + 576, :] = dot_nn(hot, whole).astype(BF16)


def weight_parts(a, b, cot, cot_far, own, one, two, three):
    for part in range(5):
        cols = slice(256 * part, 256 * part + 256)
        total = dot_tn(a, cot[:, cols]) + dot_tn(b, cot_far[:, cols])
        own[:, cols] = total[:160]
        for d, ref in ((1, one), (2, two), (3, three)):
            ref[:, cols] = total[160 * d : 160 * d + 160].astype(BF16)


def local_weight_kernel(act, act_far, cot, cot_far, own, one, two, three):
    weight_parts(act[...], act_far[...], cot, cot_far, own, one, two, three)


def group_weight_kernel(act, cot, got_far, order, own, one, two, three, cot_far):
    rows = dot_nn(order[...], got_far[...]).astype(BF16)
    cot_far[:, :640] = rows[:192]
    cot_far[:, 640:] = rows[192:]
    weight_parts(act[:192, :], act[192:, :], cot, cot_far, own, one, two, three)


def sum_of(own, *others):
    total = own[...].astype(F32)
    for other in others:
        total = total + other[...].astype(F32)
    return total


def local_sum_kernel(own, a, b, c, total):
    total[...] = sum_of(own, a, b, c)


def sum_x_kernel(local, own, a, b, c, kept, one, two, three):
    total = sum_of(own, a, b, c)
    for d, ref in enumerate((kept, one, two, three)):
        rows = slice(40 * d, 40 * d + 40)
        ref[:40, :] = local[rows, :].astype(ref.dtype)
        ref[40:, :] = total[rows].astype(ref.dtype)


def sum_y_kernel(own, a, b, c, *chunks):
    total = sum_of(own, a, b, c)
    for d, ref in enumerate(chunks):
        first = total[10 * d : 10 * d + 10]
        second = total[40 + 10 * d : 40 + 10 * d + 10]
        both = jnp.concatenate([first, second, jnp.zeros((4, 1280), F32)], axis=0)
        ref[...] = both.astype(BF16)


def sum_z_kernel(after, a, b, c, d, out):
    total = sum_of(a, b, c, d).astype(BF16)
    for i in range(8):
        out[i] = total


def final_kernel(scale, after, pieces, local, glob):
    for x in range(4):
        both = (pieces[x].astype(F32) + pieces[4 + x].astype(F32)) * scale
        local[10 * x : 10 * x + 10, :] = both[:10]
        glob[10 * x : 10 * x + 10, :] = both[10:20]


def chip(z, y, c):
    return z * 8 + y * 2 + c


def swap_cores(a):
    return lax.ppermute(a, "tok", [(i, i ^ 1) for i in range(32)])


def along_x(a, d):
    pairs = [(z * 4 + x, z * 4 + (x + d) % 4) for z in range(2) for x in range(4)]
    return lax.ppermute(a, "dp", pairs)


def along_y(a, d):
    pairs = [
        (chip(z, y, c), chip(z, (y + d) % 4, c))
        for z in range(4)
        for y in range(4)
        for c in range(2)
    ]
    return lax.ppermute(a, "tok", pairs)


def to_owner(a, d):
    pairs = []
    for z in range(4):
        to = (z + d) % 4
        for y in range(4):
            for c in range(2):
                pairs.append((chip(z, y, c), chip(2 * c + to // 2, y, to % 2)))
    return lax.ppermute(a, "tok", pairs)


CHIPS = [[chip(0, 0, c) + 2 * p for p in range(16)] for c in range(2)]


def exchange(a):
    return lax.all_to_all(
        a, "tok", split_axis=0, concat_axis=0, axis_index_groups=CHIPS, tiled=True
    )


def per_device(qkv_local, qkv_global, positions, slopes, cotangent, w_out_local, w_out_global):
    tokens = 192 * 256
    scale = float(tokens) ** (-0.5)
    dp, tok = lax.axis_index("dp"), lax.axis_index("tok")
    place = jnp.stack([dp % 4, tok // 8, (tok // 2) % 4, tok % 2]).astype(jnp.int32)
    qkv_local = qkv_local.reshape(2, 96, 3840)
    qkv_global = qkv_global.reshape(2, 96, 3840)
    cotangent = cotangent.reshape(2, 96, 1280)
    flat_cot = cotangent.reshape(192, 1280)
    positions = positions.reshape(2, 96)
    partials = [sds((160, 1280), F32)] + [sds((160, 1280), BF16)] * 3

    (other,) = call(
        far_kernel, [sds((2, 96, 1920), BF16)], place, qkv_global, smem=(0,), name="far"
    )
    far = swap_cores(other)
    (packed,) = call(
        pack_kernel,
        [sds((1536, 640), BF16)],
        place,
        qkv_global,
        far,
        cotangent,
        jnp.asarray(HOME, BF16),
        smem=(0,),
        name="pack",
    )
    got = exchange(packed)

    d_local, act_own, act_other = call(
        local_kernel,
        [sds((2, 96, 3840), BF16), sds((192, 640), BF16), sds((192, 640), BF16)],
        place,
        slopes,
        qkv_local,
        cotangent,
        w_out_local,
        positions,
        smem=(0, 1),
        scratch=[pltpu.VMEM((192, 1280), BF16)],
        flops=2 * 10**9,
        name="local",
    )
    own, one, two, three = call(
        local_weight_kernel,
        partials,
        act_own,
        swap_cores(act_other),
        flat_cot,
        swap_cores(flat_cot),
        flops=2 * 640 * 384 * 1280,
        name="local_weight",
    )
    (local_rows,) = call(
        local_sum_kernel,
        [sds((160, 1280), F32)],
        own,
        along_x(one, 1),
        along_x(two, 2),
        along_x(three, 3),
        name="local_sum_x",
    )

    got_far = swap_cores(got.reshape(16, 96, 640)[:, 72:, :]).reshape(384, 640)
    data, cot, probs, act = call(
        group_kernel,
        [
            sds((3, 2, 192, 640), BF16),
            sds((192, 1280), BF16),
            sds((24, 64, 64), F32),
            sds((384, 640), BF16),
        ],
        place,
        local_rows,
        got,
        jnp.asarray(GROUP, BF16),
        smem=(0,),
        unread=(1,),
        scratch=[pltpu.VMEM((384, 640), BF16)],
        flops=10**9,
        name="group",
    )
    own, one, two, three, cot_far = call(
        group_weight_kernel,
        partials + [sds((192, 1280), BF16)],
        act,
        cot,
        got_far,
        jnp.asarray(FAR_COT, BF16),
        flops=2 * 640 * 384 * 1280,
        name="group_weight",
    )
    a, b, c = along_x(one, 1), along_x(two, 2), along_x(three, 3)
    (back,) = call(
        group_back_kernel,
        [sds((1152, 640), BF16)],
        place,
        probs,
        data,
        cot,
        cot_far,
        w_out_global,
        jnp.asarray(BACK, BF16),
        smem=(0,),
        scratch=[pltpu.VMEM((3, 2, 192, 640), BF16)],
        flops=2 * 10**9,
        name="group_back",
    )
    returned = exchange(back)

    own, one, two, three = call(
        sum_x_kernel,
        [sds((80, 1280), F32)] + [sds((80, 1280), BF16)] * 3,
        local_rows,
        own,
        a,
        b,
        c,
        name="sum_x",
    )
    chunks = call(
        sum_y_kernel,
        [sds((24, 1280), BF16)] * 4,
        own,
        along_y(one, 1),
        along_y(two, 2),
        along_y(three, 3),
        name="sum_y",
    )
    mine, other = call(
        unpack_kernel,
        [sds((2, 96, 1920), BF16)] * 2,
        returned,
        jnp.asarray(UNPACK, BF16),
        name="unpack",
    )
    (sums,) = call(
        sum_z_kernel,
        [sds((8, 24, 1280), BF16)],
        returned,
        *[to_owner(chunk, d) for d, chunk in enumerate(chunks)],
        unread=(0,),
        name="sum_z",
    )
    pieces = lax.all_to_all(sums, "dp", split_axis=0, concat_axis=0, tiled=True)
    (d_global,) = call(
        merge_kernel,
        [sds((2, 96, 3840), BF16)],
        place,
        mine,
        swap_cores(other),
        smem=(0,),
        name="merge",
    )
    grad_local, grad_global = call(
        functools.partial(final_kernel, scale),
        [sds((40, 1280), F32), sds((40, 1280), F32)],
        d_global,
        pieces,
        unread=(0,),
        name="final",
    )
    return (
        d_local.reshape(1, 2, 96, 3840),
        d_global.reshape(1, 2, 96, 3840),
        grad_local,
        grad_global,
    )


def solution(mesh):
    placed = (
        P("dp", "tok", None, None),
        P("dp", "tok", None, None),
        P("dp", "tok", None),
        P(),
        P("dp", "tok", None, None),
        P(),
        P(),
    )
    return jax.shard_map(
        per_device,
        mesh=mesh,
        in_specs=placed,
        out_specs=(
            P("dp", "tok", None, None),
            P("dp", "tok", None, None),
            P("tok", None),
            P("tok", None),
        ),
        check_vma=False,
    )
```

```python
import functools

import jax
import jax.numpy as jnp
import numpy as np
from jax import lax
from jax.experimental import pallas as pl
from jax.experimental.pallas import tpu as pltpu
from jax.sharding import PartitionSpec as P

WC = 16
HW = 160
VMEM_LIMIT = 20 * 1024 * 1024
BF16 = jnp.bfloat16
F32 = jnp.float32


def dot_nn(a, b):
    return lax.dot_general(a, b, (((1,), (0,)), ((), ())), preferred_element_type=F32)


def dot_nt(a, b):
    return lax.dot_general(a, b, (((1,), (1,)), ((), ())), preferred_element_type=F32)


def dot_tn(a, b):
    return lax.dot_general(a, b, (((0,), (0,)), ((), ())), preferred_element_type=F32)


def order_matrix(old, new):
    sizes = dict(old)
    count = int(np.prod(list(sizes.values())))
    index = np.arange(count).reshape([s for _, s in old])
    names = [n for n, _ in old]
    moved = np.transpose(index, [names.index(n) for n in new]).reshape(-1)
    hot = np.zeros((count, count), np.float32)
    hot[np.arange(count), moved] = 1.0
    return hot


HOME = order_matrix([("s", 2), ("o", 2), ("w", 2), ("p", 8), ("t", 6)], ["p", "s", "o", "w", "t"])
GROUP = order_matrix([("p", 8), ("s", 2), ("o", 2), ("w", 2), ("t", 6)], ["s", "o", "t", "p", "w"])
FAR_COT = order_matrix([("p", 16), ("o", 2), ("w", 2), ("t", 6)], ["o", "t", "p", "w"])
BACK = order_matrix([("s", 3), ("o", 2), ("t", 6), ("p", 8), ("w", 2)], ["p", "s", "o", "w", "t"])
UNPACK = order_matrix([("p", 8), ("s", 3), ("o", 2), ("w", 2), ("t", 6)], ["s", "o", "w", "p", "t"])


def call(kernel, outs, *args, smem=(), unread=(), scratch=(), flops=0, name=None):
    specs = [
        pl.BlockSpec(
            memory_space=pltpu.SMEM if i in smem else pl.ANY if i in unread else pltpu.VMEM
        )
        for i in range(len(args))
    ]
    size = sum(int(np.prod(a.shape)) * a.dtype.itemsize for a in args)
    size += sum(int(np.prod(o.shape)) * o.dtype.itemsize for o in outs)
    return pl.pallas_call(
        kernel,
        out_shape=outs,
        in_specs=specs,
        out_specs=[pl.BlockSpec(memory_space=pltpu.VMEM) for _ in outs],
        scratch_shapes=scratch,
        compiler_params=pltpu.CompilerParams(vmem_limit_bytes=VMEM_LIMIT),
        cost_estimate=pl.CostEstimate(flops=flops, bytes_accessed=size, transcendentals=0),
        name=name,
    )(*args)


def sds(shape, dtype):
    return jax.ShapeDtypeStruct(shape, dtype)


def head_masks():
    lane = lax.broadcasted_iota(jnp.int32, (1, 256), 1)
    return [
        ((lane >= 32 * h) & (lane < 32 * h + HW)).astype(F32).astype(BF16) for h in range(4)
    ]


def side_by_side(parts):
    lane = lax.broadcasted_iota(jnp.int32, (1, 128), 1)
    tiles = [parts[0][:, :128]]
    for h in range(3):
        tiles.append(jnp.where(lane < 32 * (h + 1), parts[h][:, 128:], parts[h + 1][:, :128]))
    tiles.append(parts[3][:, 128:])
    return jnp.concatenate(tiles, axis=1)


def windows(x):
    return [x[:, 128 * h : 128 * h + 256] for h in range(4)]


def head_rows(x):
    n = x.shape[0] // 4
    return [x[n * h : n * h + n] for h in range(4)]


def against(a, b, masks):
    parts = [dot_nt(x * m, y) for x, y, m in zip(windows(a), windows(b), masks)]
    return jnp.concatenate(parts, axis=0)


def probabilities(scores):
    weights = jnp.exp(scores - jnp.max(scores, axis=-1, keepdims=True))
    return weights / jnp.sum(weights, axis=-1, keepdims=True)


def stacked(parts):
    return jnp.concatenate(parts, axis=0)


def score_gradients(probs, grad_probs):
    inner = jnp.sum(probs * grad_probs, axis=-1, keepdims=True)
    return (probs * (grad_probs - inner)).astype(BF16)


def mixture(low, v):
    parts = [dot_nn(p, x) for p, x in zip(head_rows(low), windows(v))]
    return side_by_side(parts).astype(BF16)


def gradients(low, grad_scores, q, k, g):
    scaling = HW ** (-0.5)
    low, grad_scores = head_rows(low), head_rows(grad_scores)
    dv = [dot_tn(p, x) for p, x in zip(low, windows(g))]
    dq = [dot_nn(p, x) for p, x in zip(grad_scores, windows(k))]
    dk = [dot_tn(p, x) for p, x in zip(grad_scores, windows(q))]
    return [
        (side_by_side(dq) * scaling).astype(BF16),
        (side_by_side(dk) * scaling).astype(BF16),
        side_by_side(dv).astype(BF16),
    ]


def row_order(place):
    x, zh, y = place[0], place[1], place[2]
    rem = lax.broadcasted_iota(jnp.int32, (8, 640), 1)

    def digit(value, size):
        total = jnp.zeros_like(value)
        for k in range(1, 4):
            total = total + jnp.where(value >= k * size, 1, 0)
        return total, value - total * size

    dx, rem = digit(rem, 160)
    dy, rem = digit(rem, 40)
    df, rem = digit(rem, 10)
    to = (zh + df) & 3
    return (((to >> 1) * 4 + ((y + dy) & 3)) * 2 + (to & 1)) * 40 + ((x + dx) & 3) * 10 + rem


def row_hot(place):
    lane = row_order(place)[:1]
    rows = lax.broadcasted_iota(jnp.int32, (640, 640), 0)
    return (rows == lane).astype(F32).astype(BF16)


def lanes_of(section, core):
    return pl.ds(pl.multiple_of(1280 * section + 640 * core, 128), 640)


def far_kernel(place, qkv, out):
    for s in range(3):
        for w in range(2):
            out[w, :, 640 * s : 640 * s + 640] = qkv[w, :, lanes_of(s, 1 - place[3])]


def pack_kernel(place, qkv, far, cot, order, out):
    hot = order[...]
    for group in range(2):
        rows = slice(48 * group, 48 * group + 48)

        def section(s):
            own = [qkv[w, rows, lanes_of(s, place[3])] for w in range(2)]
            return own + [far[w, rows, 640 * s : 640 * s + 640] for w in range(2)]

        cots = [cot[w, rows, 640 * half : 640 * half + 640] for half in range(2) for w in range(2)]
        for part, pieces in enumerate((section(0) + section(1), section(2) + cots)):
            sent = dot_nn(hot, jnp.concatenate(pieces, axis=0)).astype(BF16)
            for p in range(8):
                start = 96 * (8 * group + p) + 48 * part
                out[start : start + 48, :] = sent[48 * p : 48 * p + 48, :]


def unpack_kernel(got, order, mine, other):
    hot = order[...]
    for group in range(2):
        rows = dot_nn(hot, got[576 * group : 576 * group + 576, :]).astype(BF16)
        for s in range(3):
            for o, ref in enumerate((mine, other)):
                for w in range(2):
                    start = 48 * ((s * 2 + o) * 2 + w)
                    ref[w, 48 * group : 48 * group + 48, 640 * s : 640 * s + 640] = rows[
                        start : start + 48, :
                    ]


def merge_kernel(place, mine, far, out):
    for s in range(3):
        for w in range(2):
            out[w, :, lanes_of(s, place[3])] = mine[w, :, 640 * s : 640 * s + 640]
            out[w, :, lanes_of(s, 1 - place[3])] = far[w, :, 640 * s : 640 * s + 640]


def local_kernel(place, slopes, qkv, cot, weight, positions, d_out, act_own, act_other, act_all):
    masks = head_masks()
    flat = jnp.concatenate([cot[0], cot[1]], axis=0)
    g = dot_nt(flat, weight[...]).astype(BF16)
    distances = []
    for w in range(2):
        spread = jnp.broadcast_to(positions[w : w + 1, :], (96, 96))
        spread_t = spread.astype(F32).T.astype(jnp.int32)
        distances.append(
            (
                jnp.abs((spread >> 4) - (spread_t >> 4)) + jnp.abs((spread & 15) - (spread_t & 15))
            ).astype(F32)
        )
    parts = [(w, half) for w in range(2) for half in range(2)]

    def section(s):
        return [
            qkv[w, :, 1280 * s + 640 * half : 1280 * s + 640 * half + 640] for w, half in parts
        ]

    q, k, v = section(0), section(1), section(2)
    g = [g[96 * w : 96 * w + 96, 640 * half : 640 * half + 640] for w, half in parts]
    bias = stacked([slopes[4 * half + h] * distances[w] for w, half in parts for h in range(4)])
    scores = stacked([against(a, b, masks) for a, b in zip(q, k)]) * HW ** (-0.5) - bias
    grad_probs = stacked([against(a, b, masks) for a, b in zip(g, v)])
    probs = probabilities(scores)
    low = probs.astype(BF16)
    grad_scores = score_gradients(probs, grad_probs)
    for i, (w, half) in enumerate(parts):
        rows = slice(384 * i, 384 * i + 384)
        lanes = slice(640 * half, 640 * half + 640)
        act_all[96 * w : 96 * w + 96, lanes] = mixture(low[rows], v[i])
        for s, part in enumerate(gradients(low[rows], grad_scores[rows], q[i], k[i], g[i])):
            d_out[w, :, 1280 * s + 640 * half : 1280 * s + 640 * half + 640] = part
    hot = row_hot(place)
    act_own[...] = dot_nn(act_all[:, lanes_of(0, place[3])], hot).astype(BF16)
    act_other[...] = dot_nn(act_all[:, lanes_of(0, 1 - place[3])], hot).astype(BF16)


def group_kernel(place, after, after_too, after_three, got, order, data, cot, probs_out, act, act_all):
    masks = head_masks()
    hot = order[...]
    for group in range(2):
        for part in range(2):
            pieces = [
                got[96 * (8 * group + p) + 48 * part : 96 * (8 * group + p) + 48 * part + 48, :]
                for p in range(8)
            ]
            rows = dot_nn(hot, jnp.concatenate(pieces, axis=0)).astype(BF16)
            for s in range(2):
                for o in range(2):
                    for t in range(6):
                        start = 16 * ((s * 2 + o) * 6 + t)
                        piece = rows[start : start + 16, :]
                        to = slice(32 * t + 16 * group, 32 * t + 16 * group + 16)
                        if part == 1 and s == 1:
                            cot[to, 640 * o : 640 * o + 640] = piece
                        else:
                            data[2 * part + s, o, to, :] = piece
    def section(s):
        return [
            stacked([data[s, 0, 32 * t : 32 * t + 32, :], data[s, 1, 32 * t : 32 * t + 32, :]])
            for t in range(6)
        ]

    q, k, v = section(0), section(1), section(2)
    probs = probabilities(
        stacked([against(a, b, masks) for a, b in zip(q, k)]) * HW ** (-0.5)
    )
    probs_out[...] = probs
    low = probs.astype(BF16)
    for t in range(6):
        mixed = mixture(low[256 * t : 256 * t + 256], v[t])
        act_all[32 * t : 32 * t + 32, :] = mixed[:32]
        act_all[192 + 32 * t : 192 + 32 * t + 32, :] = mixed[32:]
    act[...] = dot_nn(act_all[...], row_hot(place)).astype(BF16)


def group_back_kernel(place, probs_in, data, cot, cot_far, weight, order, back, grads):
    masks = head_masks()
    hot = order[...]
    own_rows = weight[pl.ds(pl.multiple_of(640 * place[3], 128), 640), :]
    g_own = dot_nt(cot[...], own_rows).astype(BF16)
    g_far = dot_nt(cot_far[...], own_rows).astype(BF16)
    def section(s):
        return [
            stacked([data[s, 0, 32 * t : 32 * t + 32, :], data[s, 1, 32 * t : 32 * t + 32, :]])
            for t in range(6)
        ]

    q, k, v = section(0), section(1), section(2)
    g = [
        stacked([g_own[32 * t : 32 * t + 32], g_far[32 * t : 32 * t + 32]]) for t in range(6)
    ]
    probs = probs_in[...]
    low = probs.astype(BF16)
    grad_scores = score_gradients(
        probs, stacked([against(a, b, masks) for a, b in zip(g, v)])
    )
    for t in range(6):
        rows, stack = slice(32 * t, 32 * t + 32), slice(256 * t, 256 * t + 256)
        for s, part in enumerate(gradients(low[stack], grad_scores[stack], q[t], k[t], g[t])):
            grads[s, 0, rows, :] = part[:32]
            grads[s, 1, rows, :] = part[32:]
    for group in range(2):
        pieces = [
            grads[s, o, 32 * t + 16 * group : 32 * t + 16 * group + 16, :]
            for s in range(3)
            for o in range(2)
            for t in range(6)
        ]
        whole = jnp.concatenate(pieces, axis=0)
        back[576 * group : 576 * group + 576, :] = dot_nn(hot, whole).astype(BF16)


def weight_parts(a, b, cot, cot_far, own, one, two, three):
    for part in range(5):
        cols = slice(256 * part, 256 * part + 256)
        total = dot_tn(a, cot[:, cols]) + dot_tn(b, cot_far[:, cols])
        own[:, cols] = total[:160]
        for d, ref in ((1, one), (2, two), (3, three)):
            ref[:, cols] = total[160 * d : 160 * d + 160].astype(BF16)


def local_weight_kernel(act, act_far, cot, cot_far, own, one, two, three):
    weight_parts(act[...], act_far[...], cot, cot_far, own, one, two, three)


def group_weight_kernel(act, cot, got_far, order, own, one, two, three, cot_far):
    rows = dot_nn(order[...], got_far[...]).astype(BF16)
    cot_far[:, :640] = rows[:192]
    cot_far[:, 640:] = rows[192:]
    weight_parts(act[:192, :], act[192:, :], cot, cot_far, own, one, two, three)


def sum_of(own, *others):
    total = own[...].astype(F32)
    for other in others:
        total = total + other[...].astype(F32)
    return total


def sum_x_kernel(*refs):
    local, total, chunks = sum_of(*refs[:4]), sum_of(*refs[4:8]), refs[8:]
    for d, ref in enumerate(chunks):
        rows = slice(40 * d, 40 * d + 40)
        ref[:40, :] = local[rows].astype(ref.dtype)
        ref[40:, :] = total[rows].astype(ref.dtype)


def sum_y_kernel(own, a, b, c, *chunks):
    total = sum_of(own, a, b, c)
    for d, ref in enumerate(chunks):
        first = total[10 * d : 10 * d + 10]
        second = total[40 + 10 * d : 40 + 10 * d + 10]
        both = jnp.concatenate([first, second, jnp.zeros((4, 1280), F32)], axis=0)
        ref[...] = both.astype(BF16)


def sum_z_kernel(after, a, b, c, d, out):
    total = sum_of(a, b, c, d).astype(BF16)
    for i in range(8):
        out[i] = total


def final_kernel(scale, after, pieces, local, glob):
    for x in range(4):
        both = (pieces[x].astype(F32) + pieces[4 + x].astype(F32)) * scale
        local[10 * x : 10 * x + 10, :] = both[:10]
        glob[10 * x : 10 * x + 10, :] = both[10:20]


def chip(z, y, c):
    return z * 8 + y * 2 + c


def swap_cores(a):
    return lax.ppermute(a, "tok", [(i, i ^ 1) for i in range(32)])


def along_x(a, d):
    pairs = [(z * 4 + x, z * 4 + (x + d) % 4) for z in range(2) for x in range(4)]
    return lax.ppermute(a, "dp", pairs)


def along_y(a, d):
    pairs = [
        (chip(z, y, c), chip(z, (y + d) % 4, c))
        for z in range(4)
        for y in range(4)
        for c in range(2)
    ]
    return lax.ppermute(a, "tok", pairs)


def to_owner(a, d):
    pairs = []
    for z in range(4):
        to = (z + d) % 4
        for y in range(4):
            for c in range(2):
                pairs.append((chip(z, y, c), chip(2 * c + to // 2, y, to % 2)))
    return lax.ppermute(a, "tok", pairs)


CHIPS = [[chip(0, 0, c) + 2 * p for p in range(16)] for c in range(2)]


def exchange(a):
    return lax.all_to_all(
        a, "tok", split_axis=0, concat_axis=0, axis_index_groups=CHIPS, tiled=True
    )


def per_device(qkv_local, qkv_global, positions, slopes, cotangent, w_out_local, w_out_global):
    tokens = 192 * 256
    scale = float(tokens) ** (-0.5)
    dp, tok = lax.axis_index("dp"), lax.axis_index("tok")
    place = jnp.stack([dp % 4, tok // 8, (tok // 2) % 4, tok % 2]).astype(jnp.int32)
    qkv_local = qkv_local.reshape(2, 96, 3840)
    qkv_global = qkv_global.reshape(2, 96, 3840)
    cotangent = cotangent.reshape(2, 96, 1280)
    flat_cot = cotangent.reshape(192, 1280)
    positions = positions.reshape(2, 96)
    partials = [sds((160, 1280), F32)] + [sds((160, 1280), BF16)] * 3

    (other,) = call(
        far_kernel, [sds((2, 96, 1920), BF16)], place, qkv_global, smem=(0,), name="far"
    )
    far = swap_cores(other)
    (packed,) = call(
        pack_kernel,
        [sds((1536, 640), BF16)],
        place,
        qkv_global,
        far,
        cotangent,
        jnp.asarray(HOME, BF16),
        smem=(0,),
        name="pack",
    )
    got = exchange(packed)

    d_local, act_own, act_other = call(
        local_kernel,
        [sds((2, 96, 3840), BF16), sds((192, 640), BF16), sds((192, 640), BF16)],
        place,
        slopes,
        qkv_local,
        cotangent,
        w_out_local,
        positions,
        smem=(0, 1),
        scratch=[pltpu.VMEM((192, 1280), BF16)],
        flops=2 * 10**9,
        name="local",
    )
    own, one, two, three = call(
        local_weight_kernel,
        partials,
        act_own,
        swap_cores(act_other),
        flat_cot,
        swap_cores(flat_cot),
        flops=2 * 640 * 384 * 1280,
        name="local_weight",
    )
    local_parts = [own, along_x(one, 1), along_x(two, 2), along_x(three, 3)]

    got_far = swap_cores(got.reshape(16, 96, 640)[:, 72:, :]).reshape(384, 640)
    data, cot, probs, act = call(
        group_kernel,
        [
            sds((3, 2, 192, 640), BF16),
            sds((192, 1280), BF16),
            sds((1536, 64), F32),
            sds((384, 640), BF16),
        ],
        place,
        *local_parts[1:],
        got,
        jnp.asarray(GROUP, BF16),
        smem=(0,),
        unread=(1, 2, 3),
        scratch=[pltpu.VMEM((384, 640), BF16)],
        flops=10**9,
        name="group",
    )
    own, one, two, three, cot_far = call(
        group_weight_kernel,
        partials + [sds((192, 1280), BF16)],
        act,
        cot,
        got_far,
        jnp.asarray(FAR_COT, BF16),
        flops=2 * 640 * 384 * 1280,
        name="group_weight",
    )
    a, b, c = along_x(one, 1), along_x(two, 2), along_x(three, 3)
    (back,) = call(
        group_back_kernel,
        [sds((1152, 640), BF16)],
        place,
        probs,
        data,
        cot,
        cot_far,
        w_out_global,
        jnp.asarray(BACK, BF16),
        smem=(0,),
        scratch=[pltpu.VMEM((3, 2, 192, 640), BF16)],
        flops=2 * 10**9,
        name="group_back",
    )
    returned = exchange(back)

    own, one, two, three = call(
        sum_x_kernel,
        [sds((80, 1280), F32)] + [sds((80, 1280), BF16)] * 3,
        *local_parts,
        own,
        a,
        b,
        c,
        flops=10**11,
        name="sum_x",
    )
    chunks = call(
        sum_y_kernel,
        [sds((24, 1280), BF16)] * 4,
        own,
        along_y(one, 1),
        along_y(two, 2),
        along_y(three, 3),
        name="sum_y",
    )
    mine, other = call(
        unpack_kernel,
        [sds((2, 96, 1920), BF16)] * 2,
        returned,
        jnp.asarray(UNPACK, BF16),
        name="unpack",
    )
    (sums,) = call(
        sum_z_kernel,
        [sds((8, 24, 1280), BF16)],
        returned,
        *[to_owner(chunk, d) for d, chunk in enumerate(chunks)],
        unread=(0,),
        name="sum_z",
    )
    pieces = lax.all_to_all(sums, "dp", split_axis=0, concat_axis=0, tiled=True)
    (d_global,) = call(
        merge_kernel,
        [sds((2, 96, 3840), BF16)],
        place,
        mine,
        swap_cores(other),
        smem=(0,),
        name="merge",
    )
    grad_local, grad_global = call(
        functools.partial(final_kernel, scale),
        [sds((40, 1280), F32), sds((40, 1280), F32)],
        d_global,
        pieces,
        unread=(0,),
        name="final",
    )
    return (
        d_local.reshape(1, 2, 96, 3840),
        d_global.reshape(1, 2, 96, 3840),
        grad_local,
        grad_global,
    )


def solution(mesh):
    placed = (
        P("dp", "tok", None, None),
        P("dp", "tok", None, None),
        P("dp", "tok", None),
        P(),
        P("dp", "tok", None, None),
        P(),
        P(),
    )
    return jax.shard_map(
        per_device,
        mesh=mesh,
        in_specs=placed,
        out_specs=(
            P("dp", "tok", None, None),
            P("dp", "tok", None, None),
            P("tok", None),
            P("tok", None),
        ),
        check_vma=False,
    )
```

```python
import functools

import jax
import jax.numpy as jnp
from jax import lax
from jax.experimental import pallas as pl
from jax.experimental.pallas import tpu as pltpu
from jax.sharding import PartitionSpec as P

WC = 16
HW = 160
VMEM_LIMIT = 12 * 1024 * 1024
BF16 = jnp.bfloat16
F32 = jnp.float32


def dot_nn(a, b):
    return lax.dot_general(a, b, (((1,), (0,)), ((), ())), preferred_element_type=F32)


def dot_nt(a, b):
    return lax.dot_general(a, b, (((1,), (1,)), ((), ())), preferred_element_type=F32)


def dot_tn(a, b):
    return lax.dot_general(a, b, (((0,), (0,)), ((), ())), preferred_element_type=F32)


def order_matrix(old, new):
    count = 1
    for _, size in old:
        count *= size
    left = lax.broadcasted_iota(jnp.int32, (8, count), 1).astype(F32)
    digits = {}
    for name, size in reversed(old):
        whole = jnp.floor((left + 0.5) * (1.0 / size))
        digits[name], left = left - whole * size, whole
    place, sizes = jnp.zeros_like(left), dict(old)
    for name in new:
        place = place * sizes[name] + digits[name]
    rows = lax.broadcasted_iota(jnp.int32, (count, count), 0)
    return (rows == place.astype(jnp.int32)[:1]).astype(F32).astype(BF16)


HOME = ([("s", 2), ("o", 2), ("w", 2), ("p", 8), ("t", 6)], ["p", "s", "o", "w", "t"])
GROUP = ([("p", 8), ("s", 2), ("o", 2), ("w", 2), ("t", 6)], ["s", "o", "t", "p", "w"])
FAR_COT = ([("p", 16), ("o", 2), ("w", 2), ("t", 6)], ["o", "t", "p", "w"])
BACK = ([("s", 3), ("o", 2), ("t", 6), ("p", 8), ("w", 2)], ["p", "s", "o", "w", "t"])
UNPACK = ([("p", 8), ("s", 3), ("o", 2), ("w", 2), ("t", 6)], ["s", "o", "w", "p", "t"])


def call(kernel, outs, *args, smem=(), unread=(), scratch=(), flops=0, name=None):
    specs = [
        pl.BlockSpec(
            memory_space=pltpu.SMEM if i in smem else pl.ANY if i in unread else pltpu.VMEM
        )
        for i in range(len(args))
    ]
    size = sum(a.size * a.dtype.itemsize for a in args)
    size += sum(o.size * o.dtype.itemsize for o in outs)
    return pl.pallas_call(
        kernel,
        out_shape=outs,
        in_specs=specs,
        out_specs=[pl.BlockSpec(memory_space=pltpu.VMEM) for _ in outs],
        scratch_shapes=scratch,
        compiler_params=pltpu.CompilerParams(vmem_limit_bytes=VMEM_LIMIT),
        cost_estimate=pl.CostEstimate(flops=flops, bytes_accessed=size, transcendentals=0),
        name=name,
    )(*args)


def sds(shape, dtype):
    return jax.ShapeDtypeStruct(shape, dtype)


def head_masks():
    lane = lax.broadcasted_iota(jnp.int32, (1, 256), 1)
    return [
        ((lane >= 32 * h) & (lane < 32 * h + HW)).astype(F32).astype(BF16) for h in range(4)
    ]


def side_by_side(parts):
    lane = lax.broadcasted_iota(jnp.int32, (1, 128), 1)
    tiles = [parts[0][:, :128]]
    for h in range(3):
        tiles.append(jnp.where(lane < 32 * (h + 1), parts[h][:, 128:], parts[h + 1][:, :128]))
    tiles.append(parts[3][:, 128:])
    return jnp.concatenate(tiles, axis=1)


def windows(x):
    return [x[:, 128 * h : 128 * h + 256] for h in range(4)]


def head_rows(x):
    n = x.shape[0] // 4
    return [x[n * h : n * h + n] for h in range(4)]


def against(a, b, masks):
    parts = [dot_nt(x * m, y) for x, y, m in zip(windows(a), windows(b), masks)]
    return jnp.concatenate(parts, axis=0)


def probabilities(scores):
    weights = jnp.exp(scores - jnp.max(scores, axis=-1, keepdims=True))
    return weights / jnp.sum(weights, axis=-1, keepdims=True)


def stacked(parts):
    return jnp.concatenate(parts, axis=0)


def score_gradients(probs, grad_probs):
    inner = jnp.sum(probs * grad_probs, axis=-1, keepdims=True)
    return (probs * (grad_probs - inner)).astype(BF16)


def mixture(low, v):
    parts = [dot_nn(p, x) for p, x in zip(head_rows(low), windows(v))]
    return side_by_side(parts).astype(BF16)


def gradients(low, grad_scores, q, k, g):
    scaling = HW ** (-0.5)
    low, grad_scores = head_rows(low), head_rows(grad_scores)
    dv = [dot_tn(p, x) for p, x in zip(low, windows(g))]
    dq = [dot_nn(p, x) for p, x in zip(grad_scores, windows(k))]
    dk = [dot_tn(p, x) for p, x in zip(grad_scores, windows(q))]
    return [
        (side_by_side(dq) * scaling).astype(BF16),
        (side_by_side(dk) * scaling).astype(BF16),
        side_by_side(dv).astype(BF16),
    ]


def row_order(place, y_first):
    x, zh, y = place[0], place[1], place[2]
    rem = lax.broadcasted_iota(jnp.int32, (8, 640), 1)

    def digit(value, size):
        total = jnp.zeros_like(value)
        for k in range(1, 4):
            total = total + jnp.where(value >= k * size, 1, 0)
        return total, value - total * size

    first, rem = digit(rem, 160)
    second, rem = digit(rem, 40)
    dx, dy = (second, first) if y_first else (first, second)
    df, rem = digit(rem, 10)
    to = (zh + df) & 3
    return (((to >> 1) * 4 + ((y + dy) & 3)) * 2 + (to & 1)) * 40 + ((x + dx) & 3) * 10 + rem


def row_hot(place, y_first):
    lane = row_order(place, y_first)[:1]
    rows = lax.broadcasted_iota(jnp.int32, (640, 640), 0)
    return (rows == lane).astype(F32).astype(BF16)


def lanes_of(section, core):
    return pl.ds(pl.multiple_of(1280 * section + 640 * core, 128), 640)


def far_kernel(place, qkv, out):
    for s in range(3):
        for w in range(2):
            out[w, :, 640 * s : 640 * s + 640] = qkv[w, :, lanes_of(s, 1 - place[3])]


def pack_kernel(place, qkv, far, cot, out):
    hot = order_matrix(*HOME)
    for group in range(2):
        rows = slice(48 * group, 48 * group + 48)

        def section(s):
            own = [qkv[w, rows, lanes_of(s, place[3])] for w in range(2)]
            return own + [far[w, rows, 640 * s : 640 * s + 640] for w in range(2)]

        cots = [cot[w, rows, 640 * half : 640 * half + 640] for half in range(2) for w in range(2)]
        for part, pieces in enumerate((section(0) + section(1), section(2) + cots)):
            sent = dot_nn(hot, jnp.concatenate(pieces, axis=0)).astype(BF16)
            for p in range(8):
                start = 96 * (8 * group + p) + 48 * part
                out[start : start + 48, :] = sent[48 * p : 48 * p + 48, :]


def unpack_kernel(got, mine, other):
    hot = order_matrix(*UNPACK)
    for group in range(2):
        rows = dot_nn(hot, got[576 * group : 576 * group + 576, :]).astype(BF16)
        for s in range(3):
            for o, ref in enumerate((mine, other)):
                for w in range(2):
                    start = 48 * ((s * 2 + o) * 2 + w)
                    ref[w, 48 * group : 48 * group + 48, 640 * s : 640 * s + 640] = rows[
                        start : start + 48, :
                    ]


def merge_kernel(place, mine, far, out):
    for s in range(3):
        for w in range(2):
            out[w, :, lanes_of(s, place[3])] = mine[w, :, 640 * s : 640 * s + 640]
            out[w, :, lanes_of(s, 1 - place[3])] = far[w, :, 640 * s : 640 * s + 640]


def local_kernel(place, slopes, qkv, cot, weight, positions, d_out, act_own, act_other, act_all):
    masks = head_masks()
    flat = jnp.concatenate([cot[0], cot[1]], axis=0)
    g = dot_nt(flat, weight[...]).astype(BF16)
    distances = []
    for w in range(2):
        spread = jnp.broadcast_to(positions[w : w + 1, :], (96, 96))
        spread_t = spread.astype(F32).T.astype(jnp.int32)
        distances.append(
            (
                jnp.abs((spread >> 4) - (spread_t >> 4)) + jnp.abs((spread & 15) - (spread_t & 15))
            ).astype(F32)
        )
    parts = [(w, half) for w in range(2) for half in range(2)]

    def section(s):
        return [
            qkv[w, :, 1280 * s + 640 * half : 1280 * s + 640 * half + 640] for w, half in parts
        ]

    q, k, v = section(0), section(1), section(2)
    g = [g[96 * w : 96 * w + 96, 640 * half : 640 * half + 640] for w, half in parts]
    bias = stacked([slopes[4 * half + h] * distances[w] for w, half in parts for h in range(4)])
    scores = stacked([against(a, b, masks) for a, b in zip(q, k)]) * HW ** (-0.5) - bias
    grad_probs = stacked([against(a, b, masks) for a, b in zip(g, v)])
    probs = probabilities(scores)
    low = probs.astype(BF16)
    grad_scores = score_gradients(probs, grad_probs)
    for i, (w, half) in enumerate(parts):
        rows = slice(384 * i, 384 * i + 384)
        lanes = slice(640 * half, 640 * half + 640)
        act_all[96 * w : 96 * w + 96, lanes] = mixture(low[rows], v[i])
        for s, part in enumerate(gradients(low[rows], grad_scores[rows], q[i], k[i], g[i])):
            d_out[w, :, 1280 * s + 640 * half : 1280 * s + 640 * half + 640] = part
    hot = row_hot(place, False)
    act_own[...] = dot_nn(act_all[:, lanes_of(0, place[3])], hot).astype(BF16)
    act_other[...] = dot_nn(act_all[:, lanes_of(0, 1 - place[3])], hot).astype(BF16)


def group_kernel(place, after, after_too, after_three, got, data, cot, probs_out, act, act_all):
    masks = head_masks()
    hot = order_matrix(*GROUP)
    for group in range(2):
        for part in range(2):
            pieces = [
                got[96 * (8 * group + p) + 48 * part : 96 * (8 * group + p) + 48 * part + 48, :]
                for p in range(8)
            ]
            rows = dot_nn(hot, jnp.concatenate(pieces, axis=0)).astype(BF16)
            for s in range(2):
                for o in range(2):
                    for t in range(6):
                        start = 16 * ((s * 2 + o) * 6 + t)
                        piece = rows[start : start + 16, :]
                        to = slice(32 * t + 16 * group, 32 * t + 16 * group + 16)
                        if part == 1 and s == 1:
                            cot[to, 640 * o : 640 * o + 640] = piece
                        else:
                            data[2 * part + s, o, to, :] = piece
    def section(s):
        return [
            stacked([data[s, 0, 32 * t : 32 * t + 32, :], data[s, 1, 32 * t : 32 * t + 32, :]])
            for t in range(6)
        ]

    q, k, v = section(0), section(1), section(2)
    probs = probabilities(
        stacked([against(a, b, masks) for a, b in zip(q, k)]) * HW ** (-0.5)
    )
    probs_out[...] = probs
    low = probs.astype(BF16)
    for t in range(6):
        mixed = mixture(low[256 * t : 256 * t + 256], v[t])
        act_all[32 * t : 32 * t + 32, :] = mixed[:32]
        act_all[192 + 32 * t : 192 + 32 * t + 32, :] = mixed[32:]
    act[...] = dot_nn(act_all[...], row_hot(place, True)).astype(BF16)


def group_back_kernel(place, probs_in, data, cot, cot_far, weight, back, grads):
    masks = head_masks()
    hot = order_matrix(*BACK)
    own_rows = weight[pl.ds(pl.multiple_of(640 * place[3], 128), 640), :]
    g_own = dot_nt(cot[...], own_rows).astype(BF16)
    g_far = dot_nt(cot_far[...], own_rows).astype(BF16)
    def section(s):
        return [
            stacked([data[s, 0, 32 * t : 32 * t + 32, :], data[s, 1, 32 * t : 32 * t + 32, :]])
            for t in range(6)
        ]

    q, k, v = section(0), section(1), section(2)
    g = [
        stacked([g_own[32 * t : 32 * t + 32], g_far[32 * t : 32 * t + 32]]) for t in range(6)
    ]
    probs = probs_in[...]
    low = probs.astype(BF16)
    grad_scores = score_gradients(
        probs, stacked([against(a, b, masks) for a, b in zip(g, v)])
    )
    for t in range(6):
        rows, stack = slice(32 * t, 32 * t + 32), slice(256 * t, 256 * t + 256)
        for s, part in enumerate(gradients(low[stack], grad_scores[stack], q[t], k[t], g[t])):
            grads[s, 0, rows, :] = part[:32]
            grads[s, 1, rows, :] = part[32:]
    for group in range(2):
        pieces = [
            grads[s, o, 32 * t + 16 * group : 32 * t + 16 * group + 16, :]
            for s in range(3)
            for o in range(2)
            for t in range(6)
        ]
        whole = jnp.concatenate(pieces, axis=0)
        back[576 * group : 576 * group + 576, :] = dot_nn(hot, whole).astype(BF16)


def weight_parts(a, b, cot, cot_far, own, one, two, three):
    for part in range(5):
        cols = slice(256 * part, 256 * part + 256)
        total = dot_tn(a, cot[:, cols]) + dot_tn(b, cot_far[:, cols])
        own[:, cols] = total[:160]
        for d, ref in ((1, one), (2, two), (3, three)):
            ref[:, cols] = total[160 * d : 160 * d + 160].astype(BF16)


def local_weight_kernel(act, act_far, cot, cot_far, own, one, two, three):
    weight_parts(act[...], act_far[...], cot, cot_far, own, one, two, three)


def group_weight_kernel(act, cot, got_far, own, one, two, three, cot_far):
    rows = dot_nn(order_matrix(*FAR_COT), got_far[...]).astype(BF16)
    cot_far[:, :640] = rows[:192]
    cot_far[:, 640:] = rows[192:]
    weight_parts(act[:192, :], act[192:, :], cot, cot_far, own, one, two, three)


def sum_of(own, *others):
    total = own[...].astype(F32)
    for other in others:
        total = total + other[...].astype(F32)
    return total


def first_sum_kernel(own, a, b, c, *chunks):
    total = sum_of(own, a, b, c)
    for d, ref in enumerate(chunks):
        ref[...] = total[40 * d : 40 * d + 40].astype(ref.dtype)


def second_sum_kernel(*refs):
    local, total, chunks = sum_of(*refs[:4]), sum_of(*refs[4:8]), refs[8:]
    for d, ref in enumerate(chunks):
        rows = slice(10 * d, 10 * d + 10)
        both = jnp.concatenate([local[rows], total[rows], jnp.zeros((4, 1280), F32)], axis=0)
        ref[...] = both.astype(BF16)


def sum_z_kernel(after, a, b, c, d, out):
    total = sum_of(a, b, c, d).astype(BF16)
    for i in range(8):
        out[i] = total


def final_kernel(scale, after, pieces, local, glob):
    for x in range(4):
        both = (pieces[x].astype(F32) + pieces[4 + x].astype(F32)) * scale
        local[10 * x : 10 * x + 10, :] = both[:10]
        glob[10 * x : 10 * x + 10, :] = both[10:20]


def chip(z, y, c):
    return z * 8 + y * 2 + c


def swap_cores(a):
    return lax.ppermute(a, "tok", [(i, i ^ 1) for i in range(32)])


def along_x(a, d):
    pairs = [(z * 4 + x, z * 4 + (x + d) % 4) for z in range(2) for x in range(4)]
    return lax.ppermute(a, "dp", pairs)


def along_y(a, d):
    pairs = [
        (chip(z, y, c), chip(z, (y + d) % 4, c))
        for z in range(4)
        for y in range(4)
        for c in range(2)
    ]
    return lax.ppermute(a, "tok", pairs)


def to_owner(a, d):
    pairs = []
    for z in range(4):
        to = (z + d) % 4
        for y in range(4):
            for c in range(2):
                pairs.append((chip(z, y, c), chip(2 * c + to // 2, y, to % 2)))
    return lax.ppermute(a, "tok", pairs)


CHIPS = [[chip(0, 0, c) + 2 * p for p in range(16)] for c in range(2)]


def exchange(a):
    return lax.all_to_all(
        a, "tok", split_axis=0, concat_axis=0, axis_index_groups=CHIPS, tiled=True
    )


def per_device(qkv_local, qkv_global, positions, slopes, cotangent, w_out_local, w_out_global):
    tokens = 192 * 256
    scale = float(tokens) ** (-0.5)
    dp, tok = lax.axis_index("dp"), lax.axis_index("tok")
    place = jnp.stack([dp % 4, tok // 8, (tok // 2) % 4, tok % 2]).astype(jnp.int32)
    qkv_local = qkv_local.reshape(2, 96, 3840)
    qkv_global = qkv_global.reshape(2, 96, 3840)
    cotangent = cotangent.reshape(2, 96, 1280)
    flat_cot = cotangent.reshape(192, 1280)
    positions = positions.reshape(2, 96)
    first_sums = [sds((40, 1280), F32)] + [sds((40, 1280), BF16)] * 3
    partials = [sds((160, 1280), F32)] + [sds((160, 1280), BF16)] * 3

    (other,) = call(
        far_kernel, [sds((2, 96, 1920), BF16)], place, qkv_global, smem=(0,), name="far"
    )
    far = swap_cores(other)
    (packed,) = call(
        pack_kernel,
        [sds((1536, 640), BF16)],
        place,
        qkv_global,
        far,
        cotangent,
        smem=(0,),
        name="pack",
    )
    got = exchange(packed)

    d_local, act_own, act_other = call(
        local_kernel,
        [sds((2, 96, 3840), BF16), sds((192, 640), BF16), sds((192, 640), BF16)],
        place,
        slopes,
        qkv_local,
        cotangent,
        w_out_local,
        positions,
        smem=(0, 1),
        scratch=[pltpu.VMEM((192, 1280), BF16)],
        flops=2 * 10**9,
        name="local",
    )
    own, one, two, three = call(
        local_weight_kernel,
        partials,
        act_own,
        swap_cores(act_other),
        flat_cot,
        swap_cores(flat_cot),
        flops=2 * 640 * 384 * 1280,
        name="local_weight",
    )
    own, one, two, three = call(
        first_sum_kernel,
        first_sums,
        own,
        along_x(one, 1),
        along_x(two, 2),
        along_x(three, 3),
        name="local_sum_x",
    )
    local_parts = [own, along_y(one, 1), along_y(two, 2), along_y(three, 3)]

    got_far = swap_cores(got.reshape(16, 96, 640)[:, 72:, :]).reshape(384, 640)
    data, cot, probs, act = call(
        group_kernel,
        [
            sds((3, 2, 192, 640), BF16),
            sds((192, 1280), BF16),
            sds((1536, 64), F32),
            sds((384, 640), BF16),
        ],
        place,
        *local_parts[1:],
        got,
        smem=(0,),
        unread=(1, 2, 3),
        scratch=[pltpu.VMEM((384, 640), BF16)],
        flops=10**11,
        name="group",
    )
    own, one, two, three, cot_far = call(
        group_weight_kernel,
        partials + [sds((192, 1280), BF16)],
        act,
        cot,
        got_far,
        flops=2 * 640 * 384 * 1280,
        name="group_weight",
    )
    a, b, c = along_y(one, 1), along_y(two, 2), along_y(three, 3)
    (back,) = call(
        group_back_kernel,
        [sds((1152, 640), BF16)],
        place,
        probs,
        data,
        cot,
        cot_far,
        w_out_global,
        smem=(0,),
        scratch=[pltpu.VMEM((3, 2, 192, 640), BF16)],
        flops=2 * 10**9,
        name="group_back",
    )
    returned = exchange(back)

    own, one, two, three = call(
        first_sum_kernel,
        first_sums,
        own,
        a,
        b,
        c,
        flops=10**11,
        name="sum_y",
    )
    chunks = call(
        second_sum_kernel,
        [sds((24, 1280), BF16)] * 4,
        *local_parts,
        own,
        along_x(one, 1),
        along_x(two, 2),
        along_x(three, 3),
        name="sum_x",
    )
    mine, other = call(
        unpack_kernel,
        [sds((2, 96, 1920), BF16)] * 2,
        returned,
        name="unpack",
    )
    (sums,) = call(
        sum_z_kernel,
        [sds((8, 24, 1280), BF16)],
        returned,
        *[to_owner(chunk, d) for d, chunk in enumerate(chunks)],
        unread=(0,),
        name="sum_z",
    )
    pieces = lax.all_to_all(sums, "dp", split_axis=0, concat_axis=0, tiled=True)
    (d_global,) = call(
        merge_kernel,
        [sds((2, 96, 3840), BF16)],
        place,
        mine,
        swap_cores(other),
        smem=(0,),
        name="merge",
    )
    grad_local, grad_global = call(
        functools.partial(final_kernel, scale),
        [sds((40, 1280), F32), sds((40, 1280), F32)],
        d_global,
        pieces,
        unread=(0,),
        name="final",
    )
    return (
        d_local.reshape(1, 2, 96, 3840),
        d_global.reshape(1, 2, 96, 3840),
        grad_local,
        grad_global,
    )


def solution(mesh):
    placed = (
        P("dp", "tok", None, None),
        P("dp", "tok", None, None),
        P("dp", "tok", None),
        P(),
        P("dp", "tok", None, None),
        P(),
        P(),
    )
    return jax.shard_map(
        per_device,
        mesh=mesh,
        in_specs=placed,
        out_specs=(
            P("dp", "tok", None, None),
            P("dp", "tok", None, None),
            P("tok", None),
            P("tok", None),
        ),
        check_vma=False,
    )
```

```python
import functools

import jax
import jax.numpy as jnp
from jax import lax
from jax.experimental import pallas as pl
from jax.experimental.pallas import tpu as pltpu
from jax.sharding import PartitionSpec as P

WC = 16
HW = 160
VMEM_LIMIT = 12 * 1024 * 1024
BF16 = jnp.bfloat16
F32 = jnp.float32


def dot_nn(a, b):
    return lax.dot_general(a, b, (((1,), (0,)), ((), ())), preferred_element_type=F32)


def dot_nt(a, b):
    return lax.dot_general(a, b, (((1,), (1,)), ((), ())), preferred_element_type=F32)


def dot_tn(a, b):
    return lax.dot_general(a, b, (((0,), (0,)), ((), ())), preferred_element_type=F32)


def order_matrix(old, new):
    count = 1
    for _, size in old:
        count *= size
    left = lax.broadcasted_iota(jnp.int32, (8, count), 1).astype(F32)
    digits = {}
    for name, size in reversed(old):
        whole = jnp.floor((left + 0.5) * (1.0 / size))
        digits[name], left = left - whole * size, whole
    place, sizes = jnp.zeros_like(left), dict(old)
    for name in new:
        place = place * sizes[name] + digits[name]
    rows = lax.broadcasted_iota(jnp.int32, (count, count), 0)
    return (rows == place.astype(jnp.int32)[:1]).astype(F32).astype(BF16)


HOME = ([("s", 2), ("o", 2), ("w", 2), ("p", 8), ("t", 6)], ["p", "s", "o", "w", "t"])
GROUP = ([("p", 8), ("s", 2), ("o", 2), ("w", 2), ("t", 6)], ["s", "o", "t", "p", "w"])
FAR_COT = ([("p", 16), ("o", 2), ("w", 2), ("t", 6)], ["o", "t", "p", "w"])
BACK = ([("s", 3), ("o", 2), ("t", 6), ("p", 8), ("w", 2)], ["p", "s", "o", "w", "t"])
UNPACK = ([("p", 8), ("s", 3), ("o", 2), ("w", 2), ("t", 6)], ["s", "o", "w", "p", "t"])


def call(kernel, outs, *args, smem=(), unread=(), sent=False, scratch=(), flops=0, name=None):
    specs = [
        pl.BlockSpec(
            memory_space=pltpu.SMEM if i in smem else pl.ANY if i in unread else pltpu.VMEM
        )
        for i in range(len(args))
    ]
    size = sum(a.size * a.dtype.itemsize for a in args)
    size += sum(o.size * o.dtype.itemsize for o in outs)
    return pl.pallas_call(
        kernel,
        out_shape=outs,
        in_specs=specs,
        out_specs=[
            pl.BlockSpec(memory_space=pl.ANY if sent and i == 0 else pltpu.VMEM)
            for i in range(len(outs))
        ],
        scratch_shapes=scratch,
        compiler_params=pltpu.CompilerParams(vmem_limit_bytes=VMEM_LIMIT),
        cost_estimate=pl.CostEstimate(flops=flops, bytes_accessed=size, transcendentals=0),
        name=name,
    )(*args)


def sds(shape, dtype):
    return jax.ShapeDtypeStruct(shape, dtype)


def head_masks():
    lane = lax.broadcasted_iota(jnp.int32, (1, 256), 1)
    return [
        ((lane >= 32 * h) & (lane < 32 * h + HW)).astype(F32).astype(BF16) for h in range(4)
    ]


def side_by_side(parts):
    lane = lax.broadcasted_iota(jnp.int32, (1, 128), 1)
    tiles = [parts[0][:, :128]]
    for h in range(3):
        tiles.append(jnp.where(lane < 32 * (h + 1), parts[h][:, 128:], parts[h + 1][:, :128]))
    tiles.append(parts[3][:, 128:])
    return jnp.concatenate(tiles, axis=1)


def windows(x):
    return [x[:, 128 * h : 128 * h + 256] for h in range(4)]


def head_rows(x):
    n = x.shape[0] // 4
    return [x[n * h : n * h + n] for h in range(4)]


def against(a, b, masks):
    parts = [dot_nt(x * m, y) for x, y, m in zip(windows(a), windows(b), masks)]
    return jnp.concatenate(parts, axis=0)


def probabilities(scores):
    weights = jnp.exp(scores - jnp.max(scores, axis=-1, keepdims=True))
    return weights / jnp.sum(weights, axis=-1, keepdims=True)


def stacked(parts):
    return jnp.concatenate(parts, axis=0)


def score_gradients(probs, grad_probs):
    inner = jnp.sum(probs * grad_probs, axis=-1, keepdims=True)
    return (probs * (grad_probs - inner)).astype(BF16)


def mixture(low, v):
    parts = [dot_nn(p, x) for p, x in zip(head_rows(low), windows(v))]
    return side_by_side(parts).astype(BF16)


def gradients(low, grad_scores, q, k, g):
    scaling = HW ** (-0.5)
    low, grad_scores = head_rows(low), head_rows(grad_scores)
    dv = [dot_tn(p, x) for p, x in zip(low, windows(g))]
    dq = [dot_nn(p, x) for p, x in zip(grad_scores, windows(k))]
    dk = [dot_tn(p, x) for p, x in zip(grad_scores, windows(q))]
    return [
        (side_by_side(dq) * scaling).astype(BF16),
        (side_by_side(dk) * scaling).astype(BF16),
        side_by_side(dv).astype(BF16),
    ]


def row_order(place, y_first):
    x, zh, y = place[0], place[1], place[2]
    rem = lax.broadcasted_iota(jnp.int32, (8, 640), 1)

    def digit(value, size):
        total = jnp.zeros_like(value)
        for k in range(1, 4):
            total = total + jnp.where(value >= k * size, 1, 0)
        return total, value - total * size

    first, rem = digit(rem, 160)
    second, rem = digit(rem, 40)
    dx, dy = (second, first) if y_first else (first, second)
    df, rem = digit(rem, 10)
    to = (zh + df) & 3
    return (((to >> 1) * 4 + ((y + dy) & 3)) * 2 + (to & 1)) * 40 + ((x + dx) & 3) * 10 + rem


def row_hot(place, y_first):
    lane = row_order(place, y_first)[:1]
    rows = lax.broadcasted_iota(jnp.int32, (640, 640), 0)
    return (rows == lane).astype(F32).astype(BF16)


def lanes_of(section, core):
    return pl.ds(pl.multiple_of(1280 * section + 640 * core, 128), 640)


def far_kernel(place, qkv, out, sems):
    sends = [
        pltpu.make_async_copy(
            qkv.at[:, :, lanes_of(s, 1 - place[3])],
            out.at[:, :, pl.ds(640 * s, 640)],
            sems.at[s],
        )
        for s in range(3)
    ]
    for send in sends:
        send.start()
    for send in sends:
        send.wait()


def copies(held, out, sems):
    rows = out.shape[0] // 2
    return [
        pltpu.make_async_copy(held.at[i], out.at[pl.ds(rows * i, rows)], sems.at[i])
        for i in range(2)
    ]


def pack_kernel(place, qkv, far, cot, out, held, sems):
    hot = order_matrix(*HOME)
    sends = copies(held, out, sems)
    for group in range(2):
        rows = slice(48 * group, 48 * group + 48)

        def section(s):
            own = [qkv[w, rows, lanes_of(s, place[3])] for w in range(2)]
            return own + [far[w, rows, 640 * s : 640 * s + 640] for w in range(2)]

        cots = [cot[w, rows, 640 * half : 640 * half + 640] for half in range(2) for w in range(2)]
        for part, pieces in enumerate((section(0) + section(1), section(2) + cots)):
            sent = dot_nn(hot, jnp.concatenate(pieces, axis=0)).astype(BF16)
            for p in range(8):
                start = 96 * p + 48 * part
                held[group, start : start + 48, :] = sent[48 * p : 48 * p + 48, :]
        sends[group].start()
    for send in sends:
        send.wait()


def unpack_kernel(got, mine, other):
    hot = order_matrix(*UNPACK)
    for group in range(2):
        rows = dot_nn(hot, got[576 * group : 576 * group + 576, :]).astype(BF16)
        for s in range(3):
            for o, ref in enumerate((mine, other)):
                for w in range(2):
                    start = 48 * ((s * 2 + o) * 2 + w)
                    ref[w, 48 * group : 48 * group + 48, 640 * s : 640 * s + 640] = rows[
                        start : start + 48, :
                    ]


def merge_kernel(place, mine, far, out, done, sems):
    done[...] = jnp.zeros_like(done)
    sends = []
    for s in range(3):
        for i, (ref, core) in enumerate(((mine, place[3]), (far, 1 - place[3]))):
            sends.append(
                pltpu.make_async_copy(
                    ref.at[:, :, pl.ds(640 * s, 640)],
                    out.at[:, :, lanes_of(s, core)],
                    sems.at[2 * s + i],
                )
            )
    for send in sends:
        send.start()
    for send in sends:
        send.wait()


def local_kernel(place, slopes, qkv, cot, weight, positions, d_out, act_own, act_other, act_all):
    masks = head_masks()
    flat = jnp.concatenate([cot[0], cot[1]], axis=0)
    g = dot_nt(flat, weight[...]).astype(BF16)
    distances = []
    for w in range(2):
        spread = jnp.broadcast_to(positions[w : w + 1, :], (96, 96))
        spread_t = spread.astype(F32).T.astype(jnp.int32)
        distances.append(
            (
                jnp.abs((spread >> 4) - (spread_t >> 4)) + jnp.abs((spread & 15) - (spread_t & 15))
            ).astype(F32)
        )
    parts = [(w, half) for w in range(2) for half in range(2)]

    def section(s):
        return [
            qkv[w, :, 1280 * s + 640 * half : 1280 * s + 640 * half + 640] for w, half in parts
        ]

    q, k, v = section(0), section(1), section(2)
    g = [g[96 * w : 96 * w + 96, 640 * half : 640 * half + 640] for w, half in parts]
    bias = stacked([slopes[4 * half + h] * distances[w] for w, half in parts for h in range(4)])
    scores = stacked([against(a, b, masks) for a, b in zip(q, k)]) * HW ** (-0.5) - bias
    grad_probs = stacked([against(a, b, masks) for a, b in zip(g, v)])
    probs = probabilities(scores)
    low = probs.astype(BF16)
    grad_scores = score_gradients(probs, grad_probs)
    for i, (w, half) in enumerate(parts):
        rows = slice(384 * i, 384 * i + 384)
        lanes = slice(640 * half, 640 * half + 640)
        act_all[96 * w : 96 * w + 96, lanes] = mixture(low[rows], v[i])
        for s, part in enumerate(gradients(low[rows], grad_scores[rows], q[i], k[i], g[i])):
            d_out[w, :, 1280 * s + 640 * half : 1280 * s + 640 * half + 640] = part
    hot = row_hot(place, False)
    act_own[...] = dot_nn(act_all[:, lanes_of(0, place[3])], hot).astype(BF16)
    act_other[...] = dot_nn(act_all[:, lanes_of(0, 1 - place[3])], hot).astype(BF16)


def group_kernel(place, after, after_too, after_three, got, data, cot, probs_out, act, act_all):
    masks = head_masks()
    hot = order_matrix(*GROUP)
    for group in range(2):
        for part in range(2):
            pieces = [
                got[96 * (8 * group + p) + 48 * part : 96 * (8 * group + p) + 48 * part + 48, :]
                for p in range(8)
            ]
            rows = dot_nn(hot, jnp.concatenate(pieces, axis=0)).astype(BF16)
            for s in range(2):
                for o in range(2):
                    for t in range(6):
                        start = 16 * ((s * 2 + o) * 6 + t)
                        piece = rows[start : start + 16, :]
                        to = slice(32 * t + 16 * group, 32 * t + 16 * group + 16)
                        if part == 1 and s == 1:
                            cot[to, 640 * o : 640 * o + 640] = piece
                        else:
                            data[2 * part + s, o, to, :] = piece
    def section(s):
        return [
            stacked([data[s, 0, 32 * t : 32 * t + 32, :], data[s, 1, 32 * t : 32 * t + 32, :]])
            for t in range(6)
        ]

    q, k, v = section(0), section(1), section(2)
    probs = probabilities(
        stacked([against(a, b, masks) for a, b in zip(q, k)]) * HW ** (-0.5)
    )
    probs_out[...] = probs
    low = probs.astype(BF16)
    for t in range(6):
        mixed = mixture(low[256 * t : 256 * t + 256], v[t])
        act_all[32 * t : 32 * t + 32, :] = mixed[:32]
        act_all[192 + 32 * t : 192 + 32 * t + 32, :] = mixed[32:]
    act[...] = dot_nn(act_all[...], row_hot(place, True)).astype(BF16)


def group_back_kernel(place, probs_in, data, cot, cot_far, weight, back, grads, held, sems):
    masks = head_masks()
    hot = order_matrix(*BACK)
    sends = copies(held, back, sems)
    own_rows = weight[pl.ds(pl.multiple_of(640 * place[3], 128), 640), :]
    g_own = dot_nt(cot[...], own_rows).astype(BF16)
    g_far = dot_nt(cot_far[...], own_rows).astype(BF16)
    def section(s):
        return [
            stacked([data[s, 0, 32 * t : 32 * t + 32, :], data[s, 1, 32 * t : 32 * t + 32, :]])
            for t in range(6)
        ]

    q, k, v = section(0), section(1), section(2)
    g = [
        stacked([g_own[32 * t : 32 * t + 32], g_far[32 * t : 32 * t + 32]]) for t in range(6)
    ]
    probs = probs_in[...]
    low = probs.astype(BF16)
    grad_scores = score_gradients(
        probs, stacked([against(a, b, masks) for a, b in zip(g, v)])
    )
    for t in range(6):
        rows, stack = slice(32 * t, 32 * t + 32), slice(256 * t, 256 * t + 256)
        for s, part in enumerate(gradients(low[stack], grad_scores[stack], q[t], k[t], g[t])):
            grads[s, 0, rows, :] = part[:32]
            grads[s, 1, rows, :] = part[32:]
    for group in range(2):
        pieces = [
            grads[s, o, 32 * t + 16 * group : 32 * t + 16 * group + 16, :]
            for s in range(3)
            for o in range(2)
            for t in range(6)
        ]
        whole = jnp.concatenate(pieces, axis=0)
        held[group] = dot_nn(hot, whole).astype(BF16)
        sends[group].start()
    for send in sends:
        send.wait()


def weight_parts(a, b, cot, cot_far, own, one, two, three):
    for part in range(5):
        cols = slice(256 * part, 256 * part + 256)
        total = dot_tn(a, cot[:, cols]) + dot_tn(b, cot_far[:, cols])
        own[:, cols] = total[:160]
        for d, ref in ((1, one), (2, two), (3, three)):
            ref[:, cols] = total[160 * d : 160 * d + 160].astype(BF16)


def local_weight_kernel(act, act_far, cot, cot_far, own, one, two, three):
    weight_parts(act[...], act_far[...], cot, cot_far, own, one, two, three)


def group_weight_kernel(act, cot, got_far, own, one, two, three, cot_far):
    rows = dot_nn(order_matrix(*FAR_COT), got_far[...]).astype(BF16)
    cot_far[:, :640] = rows[:192]
    cot_far[:, 640:] = rows[192:]
    weight_parts(act[:192, :], act[192:, :], cot, cot_far, own, one, two, three)


def sum_of(own, *others):
    total = own[...].astype(F32)
    for other in others:
        total = total + other[...].astype(F32)
    return total


def first_sum_kernel(own, a, b, c, *chunks):
    total = sum_of(own, a, b, c)
    for d, ref in enumerate(chunks):
        ref[...] = total[40 * d : 40 * d + 40].astype(ref.dtype)


def second_sum_kernel(*refs):
    local, total, chunks = sum_of(*refs[:4]), sum_of(*refs[4:8]), refs[8:]
    for d, ref in enumerate(chunks):
        rows = slice(10 * d, 10 * d + 10)
        both = jnp.concatenate([local[rows], total[rows], jnp.zeros((4, 1280), F32)], axis=0)
        ref[...] = both.astype(BF16)


def sum_z_kernel(after, a, b, c, d, out):
    total = sum_of(a, b, c, d).astype(BF16)
    for i in range(8):
        out[i] = total


def final_kernel(scale, after, pieces, local, glob):
    for x in range(4):
        both = (pieces[x].astype(F32) + pieces[4 + x].astype(F32)) * scale
        local[10 * x : 10 * x + 10, :] = both[:10]
        glob[10 * x : 10 * x + 10, :] = both[10:20]


def chip(z, y, c):
    return z * 8 + y * 2 + c


def swap_cores(a):
    return lax.ppermute(a, "tok", [(i, i ^ 1) for i in range(32)])


def along_x(a, d):
    pairs = [(z * 4 + x, z * 4 + (x + d) % 4) for z in range(2) for x in range(4)]
    return lax.ppermute(a, "dp", pairs)


def along_y(a, d):
    pairs = [
        (chip(z, y, c), chip(z, (y + d) % 4, c))
        for z in range(4)
        for y in range(4)
        for c in range(2)
    ]
    return lax.ppermute(a, "tok", pairs)


def to_owner(a, d):
    pairs = []
    for z in range(4):
        to = (z + d) % 4
        for y in range(4):
            for c in range(2):
                pairs.append((chip(z, y, c), chip(2 * c + to // 2, y, to % 2)))
    return lax.ppermute(a, "tok", pairs)


CHIPS = [[chip(i % 4, (i // 4 + i) % 4, c) for i in range(16)] for c in range(2)]


def exchange(a):
    return lax.all_to_all(
        a, "tok", split_axis=0, concat_axis=0, axis_index_groups=CHIPS, tiled=True
    )


def per_device(qkv_local, qkv_global, positions, slopes, cotangent, w_out_local, w_out_global):
    tokens = 192 * 256
    scale = float(tokens) ** (-0.5)
    dp, tok = lax.axis_index("dp"), lax.axis_index("tok")
    place = jnp.stack([dp % 4, tok // 8, (tok // 2) % 4, tok % 2]).astype(jnp.int32)
    qkv_local = qkv_local.reshape(2, 96, 3840)
    qkv_global = qkv_global.reshape(2, 96, 3840)
    cotangent = cotangent.reshape(2, 96, 1280)
    flat_cot = cotangent.reshape(192, 1280)
    positions = positions.reshape(2, 96)
    first_sums = [sds((40, 1280), F32)] + [sds((40, 1280), BF16)] * 3
    partials = [sds((160, 1280), F32)] + [sds((160, 1280), BF16)] * 3

    (other,) = call(
        far_kernel,
        [sds((2, 96, 1920), BF16)],
        place,
        qkv_global,
        smem=(0,),
        unread=(1,),
        sent=True,
        scratch=[pltpu.SemaphoreType.DMA((3,))],
        name="far",
    )
    far = swap_cores(other)
    (packed,) = call(
        pack_kernel,
        [sds((1536, 640), BF16)],
        place,
        qkv_global,
        far,
        cotangent,
        smem=(0,),
        sent=True,
        scratch=[pltpu.VMEM((2, 768, 640), BF16), pltpu.SemaphoreType.DMA((2,))],
        name="pack",
    )
    got = exchange(packed)

    d_local, act_own, act_other = call(
        local_kernel,
        [sds((2, 96, 3840), BF16), sds((192, 640), BF16), sds((192, 640), BF16)],
        place,
        slopes,
        qkv_local,
        cotangent,
        w_out_local,
        positions,
        smem=(0, 1),
        scratch=[pltpu.VMEM((192, 1280), BF16)],
        flops=2 * 10**9,
        name="local",
    )
    own, one, two, three = call(
        local_weight_kernel,
        partials,
        act_own,
        swap_cores(act_other),
        flat_cot,
        swap_cores(flat_cot),
        flops=2 * 640 * 384 * 1280,
        name="local_weight",
    )
    own, one, two, three = call(
        first_sum_kernel,
        first_sums,
        own,
        along_x(one, 1),
        along_x(two, 2),
        along_x(three, 3),
        name="local_sum_x",
    )
    local_parts = [own, along_y(one, 1), along_y(two, 2), along_y(three, 3)]

    got_far = swap_cores(got.reshape(16, 96, 640)[:, 72:, :]).reshape(384, 640)
    data, cot, probs, act = call(
        group_kernel,
        [
            sds((3, 2, 192, 640), BF16),
            sds((192, 1280), BF16),
            sds((1536, 64), F32),
            sds((384, 640), BF16),
        ],
        place,
        *local_parts[1:],
        got,
        smem=(0,),
        unread=(1, 2, 3),
        scratch=[pltpu.VMEM((384, 640), BF16)],
        flops=10**11,
        name="group",
    )
    own, one, two, three, cot_far = call(
        group_weight_kernel,
        partials + [sds((192, 1280), BF16)],
        act,
        cot,
        got_far,
        flops=2 * 640 * 384 * 1280,
        name="group_weight",
    )
    a, b, c = along_y(one, 1), along_y(two, 2), along_y(three, 3)
    (back,) = call(
        group_back_kernel,
        [sds((1152, 640), BF16)],
        place,
        probs,
        data,
        cot,
        cot_far,
        w_out_global,
        smem=(0,),
        sent=True,
        scratch=[
            pltpu.VMEM((3, 2, 192, 640), BF16),
            pltpu.VMEM((2, 576, 640), BF16),
            pltpu.SemaphoreType.DMA((2,)),
        ],
        flops=2 * 10**9,
        name="group_back",
    )
    returned = exchange(back)

    own, one, two, three = call(
        first_sum_kernel,
        first_sums,
        own,
        a,
        b,
        c,
        flops=10**11,
        name="sum_y",
    )
    chunks = call(
        second_sum_kernel,
        [sds((24, 1280), BF16)] * 4,
        *local_parts,
        own,
        along_x(one, 1),
        along_x(two, 2),
        along_x(three, 3),
        name="sum_x",
    )
    mine, other = call(
        unpack_kernel,
        [sds((2, 96, 1920), BF16)] * 2,
        returned,
        name="unpack",
    )
    (sums,) = call(
        sum_z_kernel,
        [sds((8, 24, 1280), BF16)],
        mine,
        *[to_owner(chunk, d) for d, chunk in enumerate(chunks)],
        unread=(0,),
        name="sum_z",
    )
    pieces = lax.all_to_all(sums, "dp", split_axis=0, concat_axis=0, tiled=True)
    d_global, done = call(
        merge_kernel,
        [sds((2, 96, 3840), BF16), sds((8, 128), F32)],
        place,
        mine,
        swap_cores(other),
        smem=(0,),
        unread=(1, 2),
        sent=True,
        scratch=[pltpu.SemaphoreType.DMA((6,))],
        name="merge",
    )
    grad_local, grad_global = call(
        functools.partial(final_kernel, scale),
        [sds((40, 1280), F32), sds((40, 1280), F32)],
        done,
        pieces,
        unread=(0,),
        name="final",
    )
    return (
        d_local.reshape(1, 2, 96, 3840),
        d_global.reshape(1, 2, 96, 3840),
        grad_local,
        grad_global,
    )


def solution(mesh):
    placed = (
        P("dp", "tok", None, None),
        P("dp", "tok", None, None),
        P("dp", "tok", None),
        P(),
        P("dp", "tok", None, None),
        P(),
        P(),
    )
    return jax.shard_map(
        per_device,
        mesh=mesh,
        in_specs=placed,
        out_specs=(
            P("dp", "tok", None, None),
            P("dp", "tok", None, None),
            P("tok", None),
            P("tok", None),
        ),
        check_vma=False,
    )
```

```python
import functools

import jax
import jax.numpy as jnp
from jax import lax
from jax.experimental import pallas as pl
from jax.experimental.pallas import tpu as pltpu
from jax.sharding import PartitionSpec as P

WC = 16
HW = 160
VMEM_LIMIT = 12 * 1024 * 1024
BF16 = jnp.bfloat16
F32 = jnp.float32


def dot_nn(a, b):
    return lax.dot_general(a, b, (((1,), (0,)), ((), ())), preferred_element_type=F32)


def dot_nt(a, b):
    return lax.dot_general(a, b, (((1,), (1,)), ((), ())), preferred_element_type=F32)


def dot_tn(a, b):
    return lax.dot_general(a, b, (((0,), (0,)), ((), ())), preferred_element_type=F32)


def order_matrix(old, new):
    count = 1
    for _, size in old:
        count *= size
    left = lax.broadcasted_iota(jnp.int32, (8, count), 1).astype(F32)
    digits = {}
    for name, size in reversed(old):
        whole = jnp.floor((left + 0.5) * (1.0 / size))
        digits[name], left = left - whole * size, whole
    place, sizes = jnp.zeros_like(left), dict(old)
    for name in new:
        place = place * sizes[name] + digits[name]
    rows = lax.broadcasted_iota(jnp.int32, (count, count), 0)
    return (rows == place.astype(jnp.int32)[:1]).astype(F32).astype(BF16)


HOME = ([("s", 2), ("o", 2), ("w", 2), ("p", 8), ("t", 6)], ["p", "s", "o", "w", "t"])
GROUP = ([("p", 8), ("s", 2), ("o", 2), ("w", 2), ("t", 6)], ["s", "o", "t", "p", "w"])
FAR_COT = ([("p", 16), ("o", 2), ("w", 2), ("t", 6)], ["o", "t", "p", "w"])
BACK = ([("s", 3), ("o", 2), ("t", 6), ("p", 8), ("w", 2)], ["p", "s", "o", "w", "t"])
UNPACK = ([("p", 8), ("s", 3), ("o", 2), ("w", 2), ("t", 6)], ["s", "o", "w", "p", "t"])


def call(kernel, outs, *args, smem=(), unread=(), sent=False, scratch=(), flops=0, name=None):
    specs = [
        pl.BlockSpec(
            memory_space=pltpu.SMEM if i in smem else pl.ANY if i in unread else pltpu.VMEM
        )
        for i in range(len(args))
    ]
    size = sum(a.size * a.dtype.itemsize for a in args)
    size += sum(o.size * o.dtype.itemsize for o in outs)
    return pl.pallas_call(
        kernel,
        out_shape=outs,
        in_specs=specs,
        out_specs=[
            pl.BlockSpec(memory_space=pl.ANY if sent and i == 0 else pltpu.VMEM)
            for i in range(len(outs))
        ],
        scratch_shapes=scratch,
        compiler_params=pltpu.CompilerParams(vmem_limit_bytes=VMEM_LIMIT),
        cost_estimate=pl.CostEstimate(flops=flops, bytes_accessed=size, transcendentals=0),
        name=name,
    )(*args)


def sds(shape, dtype):
    return jax.ShapeDtypeStruct(shape, dtype)


def head_masks():
    lane = lax.broadcasted_iota(jnp.int32, (1, 256), 1)
    return [
        ((lane >= 32 * h) & (lane < 32 * h + HW)).astype(F32).astype(BF16) for h in range(4)
    ]


def side_by_side(parts):
    lane = lax.broadcasted_iota(jnp.int32, (1, 128), 1)
    tiles = [parts[0][:, :128]]
    for h in range(3):
        tiles.append(jnp.where(lane < 32 * (h + 1), parts[h][:, 128:], parts[h + 1][:, :128]))
    tiles.append(parts[3][:, 128:])
    return jnp.concatenate(tiles, axis=1)


def windows(x):
    return [x[:, 128 * h : 128 * h + 256] for h in range(4)]


def head_rows(x):
    n = x.shape[0] // 4
    return [x[n * h : n * h + n] for h in range(4)]


def against(a, b, masks):
    parts = [dot_nt(x * m, y) for x, y, m in zip(windows(a), windows(b), masks)]
    return jnp.concatenate(parts, axis=0)


def probabilities(scores):
    weights = jnp.exp(scores - jnp.max(scores, axis=-1, keepdims=True))
    return weights / jnp.sum(weights, axis=-1, keepdims=True)


def stacked(parts):
    return jnp.concatenate(parts, axis=0)


def score_gradients(probs, grad_probs):
    inner = jnp.sum(probs * grad_probs, axis=-1, keepdims=True)
    return (probs * (grad_probs - inner)).astype(BF16)


def mixture(low, v):
    parts = [dot_nn(p, x) for p, x in zip(head_rows(low), windows(v))]
    return side_by_side(parts).astype(BF16)


def gradients(low, grad_scores, q, k, g):
    scaling = HW ** (-0.5)
    low, grad_scores = head_rows(low), head_rows(grad_scores)
    dv = [dot_tn(p, x) for p, x in zip(low, windows(g))]
    dq = [dot_nn(p, x) for p, x in zip(grad_scores, windows(k))]
    dk = [dot_tn(p, x) for p, x in zip(grad_scores, windows(q))]
    return [
        (side_by_side(dq) * scaling).astype(BF16),
        (side_by_side(dk) * scaling).astype(BF16),
        side_by_side(dv).astype(BF16),
    ]


def row_order(place, y_first):
    x, zh, y = place[0], place[1], place[2]
    rem = lax.broadcasted_iota(jnp.int32, (8, 640), 1)

    def digit(value, size):
        total = jnp.zeros_like(value)
        for k in range(1, 4):
            total = total + jnp.where(value >= k * size, 1, 0)
        return total, value - total * size

    first, rem = digit(rem, 160)
    second, rem = digit(rem, 40)
    dx, dy = (second, first) if y_first else (first, second)
    df, rem = digit(rem, 10)
    to = (zh + df) & 3
    return (((to >> 1) * 4 + ((y + dy) & 3)) * 2 + (to & 1)) * 40 + ((x + dx) & 3) * 10 + rem


def row_hot(place, y_first):
    lane = row_order(place, y_first)[:1]
    rows = lax.broadcasted_iota(jnp.int32, (640, 640), 0)
    return (rows == lane).astype(F32).astype(BF16)


def lanes_of(section, core):
    return pl.ds(pl.multiple_of(1280 * section + 640 * core, 128), 640)


def far_kernel(place, qkv, out, sems):
    sends = [
        pltpu.make_async_copy(
            qkv.at[:, :, lanes_of(s, 1 - place[3])],
            out.at[:, :, pl.ds(640 * s, 640)],
            sems.at[s],
        )
        for s in range(3)
    ]
    for send in sends:
        send.start()
    for send in sends:
        send.wait()


def copies(held, out, sems):
    rows = out.shape[0] // 2
    return [
        pltpu.make_async_copy(held.at[i], out.at[pl.ds(rows * i, rows)], sems.at[i])
        for i in range(2)
    ]


def pack_kernel(place, qkv, far, cot, out, held, sems):
    hot = order_matrix(*HOME)
    sends = copies(held, out, sems)
    for group in range(2):
        rows = slice(48 * group, 48 * group + 48)

        def section(s):
            own = [qkv[w, rows, lanes_of(s, place[3])] for w in range(2)]
            return own + [far[w, rows, 640 * s : 640 * s + 640] for w in range(2)]

        cots = [cot[w, rows, 640 * half : 640 * half + 640] for half in range(2) for w in range(2)]
        for part, pieces in enumerate((section(0) + section(1), section(2) + cots)):
            sent = dot_nn(hot, jnp.concatenate(pieces, axis=0)).astype(BF16)
            for p in range(8):
                start = 96 * p + 48 * part
                held[group, start : start + 48, :] = sent[48 * p : 48 * p + 48, :]
        sends[group].start()
    for send in sends:
        send.wait()


def unpack_kernel(got, mine, other):
    hot = order_matrix(*UNPACK)
    for group in range(2):
        rows = dot_nn(hot, got[576 * group : 576 * group + 576, :]).astype(BF16)
        for s in range(3):
            for o, ref in enumerate((mine, other)):
                for w in range(2):
                    start = 48 * ((s * 2 + o) * 2 + w)
                    ref[w, 48 * group : 48 * group + 48, 640 * s : 640 * s + 640] = rows[
                        start : start + 48, :
                    ]


def merge_kernel(place, mine, far, out, done, sems):
    done[...] = jnp.zeros_like(done)
    sends = []
    for s in range(3):
        for i, (ref, core) in enumerate(((mine, place[3]), (far, 1 - place[3]))):
            sends.append(
                pltpu.make_async_copy(
                    ref.at[:, :, pl.ds(640 * s, 640)],
                    out.at[:, :, lanes_of(s, core)],
                    sems.at[2 * s + i],
                )
            )
    for send in sends:
        send.start()
    for send in sends:
        send.wait()


def local_kernel(place, slopes, qkv, cot, weight, positions, d_out, act_own, act_other, act_all):
    masks = head_masks()
    flat = jnp.concatenate([cot[0], cot[1]], axis=0)
    g = dot_nt(flat, weight[...]).astype(BF16)
    distances = []
    for w in range(2):
        spread = jnp.broadcast_to(positions[w : w + 1, :], (96, 96))
        spread_t = spread.astype(F32).T.astype(jnp.int32)
        distances.append(
            (
                jnp.abs((spread >> 4) - (spread_t >> 4)) + jnp.abs((spread & 15) - (spread_t & 15))
            ).astype(F32)
        )
    parts = [(w, half) for w in range(2) for half in range(2)]

    def section(s):
        return [
            qkv[w, :, 1280 * s + 640 * half : 1280 * s + 640 * half + 640] for w, half in parts
        ]

    q, k, v = section(0), section(1), section(2)
    g = [g[96 * w : 96 * w + 96, 640 * half : 640 * half + 640] for w, half in parts]
    bias = stacked([slopes[4 * half + h] * distances[w] for w, half in parts for h in range(4)])
    scores = stacked([against(a, b, masks) for a, b in zip(q, k)]) * HW ** (-0.5) - bias
    grad_probs = stacked([against(a, b, masks) for a, b in zip(g, v)])
    probs = probabilities(scores)
    low = probs.astype(BF16)
    grad_scores = score_gradients(probs, grad_probs)
    for i, (w, half) in enumerate(parts):
        rows = slice(384 * i, 384 * i + 384)
        lanes = slice(640 * half, 640 * half + 640)
        act_all[96 * w : 96 * w + 96, lanes] = mixture(low[rows], v[i])
        for s, part in enumerate(gradients(low[rows], grad_scores[rows], q[i], k[i], g[i])):
            d_out[w, :, 1280 * s + 640 * half : 1280 * s + 640 * half + 640] = part
    hot = row_hot(place, False)
    act_own[...] = dot_nn(act_all[:, lanes_of(0, place[3])], hot).astype(BF16)
    act_other[...] = dot_nn(act_all[:, lanes_of(0, 1 - place[3])], hot).astype(BF16)


def group_kernel(place, after, after_too, after_three, got, data, cot, probs_out, act, act_all):
    masks = head_masks()
    hot = order_matrix(*GROUP)
    for group in range(2):
        for part in range(2):
            pieces = [
                got[96 * (8 * group + p) + 48 * part : 96 * (8 * group + p) + 48 * part + 48, :]
                for p in range(8)
            ]
            rows = dot_nn(hot, jnp.concatenate(pieces, axis=0)).astype(BF16)
            for s in range(2):
                for o in range(2):
                    for t in range(6):
                        start = 16 * ((s * 2 + o) * 6 + t)
                        piece = rows[start : start + 16, :]
                        to = slice(32 * t + 16 * group, 32 * t + 16 * group + 16)
                        if part == 1 and s == 1:
                            cot[to, 640 * o : 640 * o + 640] = piece
                        else:
                            data[2 * part + s, o, to, :] = piece
    def section(s):
        return [
            stacked([data[s, 0, 32 * t : 32 * t + 32, :], data[s, 1, 32 * t : 32 * t + 32, :]])
            for t in range(6)
        ]

    q, k, v = section(0), section(1), section(2)
    probs = probabilities(
        stacked([against(a, b, masks) for a, b in zip(q, k)]) * HW ** (-0.5)
    )
    probs_out[...] = probs
    low = probs.astype(BF16)
    for t in range(6):
        mixed = mixture(low[256 * t : 256 * t + 256], v[t])
        act_all[32 * t : 32 * t + 32, :] = mixed[:32]
        act_all[192 + 32 * t : 192 + 32 * t + 32, :] = mixed[32:]
    act[...] = dot_nn(act_all[...], row_hot(place, True)).astype(BF16)


def group_back_kernel(place, probs_in, data, cot, cot_far, weight, back, grads, held, sems):
    masks = head_masks()
    hot = order_matrix(*BACK)
    sends = copies(held, back, sems)
    own_rows = weight[pl.ds(pl.multiple_of(640 * place[3], 128), 640), :]
    g_own = dot_nt(cot[...], own_rows).astype(BF16)
    g_far = dot_nt(cot_far[...], own_rows).astype(BF16)
    def section(s):
        return [
            stacked([data[s, 0, 32 * t : 32 * t + 32, :], data[s, 1, 32 * t : 32 * t + 32, :]])
            for t in range(6)
        ]

    q, k, v = section(0), section(1), section(2)
    g = [
        stacked([g_own[32 * t : 32 * t + 32], g_far[32 * t : 32 * t + 32]]) for t in range(6)
    ]
    probs = probs_in[...]
    low = probs.astype(BF16)
    grad_scores = score_gradients(
        probs, stacked([against(a, b, masks) for a, b in zip(g, v)])
    )
    for t in range(6):
        rows, stack = slice(32 * t, 32 * t + 32), slice(256 * t, 256 * t + 256)
        for s, part in enumerate(gradients(low[stack], grad_scores[stack], q[t], k[t], g[t])):
            grads[s, 0, rows, :] = part[:32]
            grads[s, 1, rows, :] = part[32:]
    for group in range(2):
        pieces = [
            grads[s, o, 32 * t + 16 * group : 32 * t + 16 * group + 16, :]
            for s in range(3)
            for o in range(2)
            for t in range(6)
        ]
        whole = jnp.concatenate(pieces, axis=0)
        held[group] = dot_nn(hot, whole).astype(BF16)
        sends[group].start()
    for send in sends:
        send.wait()


def weight_parts(a, b, cot, cot_far, own, one, two, three):
    for part in range(5):
        cols = slice(256 * part, 256 * part + 256)
        total = dot_tn(a, cot[:, cols]) + dot_tn(b, cot_far[:, cols])
        own[:, cols] = total[:160]
        for d, ref in ((1, one), (2, two), (3, three)):
            ref[:, cols] = total[160 * d : 160 * d + 160].astype(BF16)


def local_weight_kernel(act, act_far, cot, cot_far, own, one, two, three):
    weight_parts(act[...], act_far[...], cot, cot_far, own, one, two, three)


def group_weight_kernel(act, cot, got_far, own, one, two, three, cot_far):
    rows = dot_nn(order_matrix(*FAR_COT), got_far[...]).astype(BF16)
    cot_far[:, :640] = rows[:192]
    cot_far[:, 640:] = rows[192:]
    weight_parts(act[:192, :], act[192:, :], cot, cot_far, own, one, two, three)


def sum_of(own, *others):
    total = own[...].astype(F32)
    for other in others:
        total = total + other[...].astype(F32)
    return total


def folded(x):
    return jnp.concatenate([x[:, :640], x[:, 640:]], axis=0)


def first_sum_kernel(own, a, b, c, *chunks):
    total = sum_of(own, a, b, c)
    for d, ref in enumerate(chunks):
        ref[...] = folded(total[40 * d : 40 * d + 40]).astype(ref.dtype)


def second_sum_kernel(*refs):
    local, total, chunks = sum_of(*refs[:4]), sum_of(*refs[4:8]), refs[8:]
    blank = jnp.zeros((4, 640), F32)
    for d, ref in enumerate(chunks):
        pieces = []
        for half in range(2):
            rows = slice(40 * half + 10 * d, 40 * half + 10 * d + 10)
            pieces += [local[rows], total[rows], blank]
        ref[...] = jnp.concatenate(pieces, axis=0).astype(BF16)


def sum_z_kernel(after, a, b, c, d, out):
    total = sum_of(a, b, c, d).astype(BF16)
    for i in range(8):
        out[i] = total


def final_kernel(scale, after, pieces, local, glob):
    for x in range(4):
        both = (pieces[x].astype(F32) + pieces[4 + x].astype(F32)) * scale
        for half in range(2):
            cols, top = slice(640 * half, 640 * half + 640), 24 * half
            local[10 * x : 10 * x + 10, cols] = both[top : top + 10]
            glob[10 * x : 10 * x + 10, cols] = both[top + 10 : top + 20]


def chip(z, y, c):
    return z * 8 + y * 2 + c


def swap_cores(a):
    return lax.ppermute(a, "tok", [(i, i ^ 1) for i in range(32)])


def along_x(a, d):
    pairs = [(z * 4 + x, z * 4 + (x + d) % 4) for z in range(2) for x in range(4)]
    return lax.ppermute(a, "dp", pairs)


def along_y(a, d):
    pairs = [
        (chip(z, y, c), chip(z, (y + d) % 4, c))
        for z in range(4)
        for y in range(4)
        for c in range(2)
    ]
    return lax.ppermute(a, "tok", pairs)


def to_owner(a, d):
    pairs = []
    for z in range(4):
        to = (z + d) % 4
        for y in range(4):
            for c in range(2):
                pairs.append((chip(z, y, c), chip(2 * c + to // 2, y, to % 2)))
    return lax.ppermute(a, "tok", pairs)


CHIPS = [[chip(i % 4, (i // 4 + i) % 4, c) for i in range(16)] for c in range(2)]


def exchange(a):
    return lax.all_to_all(
        a, "tok", split_axis=0, concat_axis=0, axis_index_groups=CHIPS, tiled=True
    )


def per_device(qkv_local, qkv_global, positions, slopes, cotangent, w_out_local, w_out_global):
    tokens = 192 * 256
    scale = float(tokens) ** (-0.5)
    dp, tok = lax.axis_index("dp"), lax.axis_index("tok")
    place = jnp.stack([dp % 4, tok // 8, (tok // 2) % 4, tok % 2]).astype(jnp.int32)
    qkv_local = qkv_local.reshape(2, 96, 3840)
    qkv_global = qkv_global.reshape(2, 96, 3840)
    cotangent = cotangent.reshape(2, 96, 1280)
    flat_cot = cotangent.reshape(192, 1280)
    positions = positions.reshape(2, 96)
    first_sums = [sds((80, 640), F32)] + [sds((80, 640), BF16)] * 3
    partials = [sds((160, 1280), F32)] + [sds((160, 1280), BF16)] * 3

    (other,) = call(
        far_kernel,
        [sds((2, 96, 1920), BF16)],
        place,
        qkv_global,
        smem=(0,),
        unread=(1,),
        sent=True,
        scratch=[pltpu.SemaphoreType.DMA((3,))],
        name="far",
    )
    far = swap_cores(other)
    (packed,) = call(
        pack_kernel,
        [sds((1536, 640), BF16)],
        place,
        qkv_global,
        far,
        cotangent,
        smem=(0,),
        sent=True,
        scratch=[pltpu.VMEM((2, 768, 640), BF16), pltpu.SemaphoreType.DMA((2,))],
        name="pack",
    )
    got = exchange(packed)

    d_local, act_own, act_other = call(
        local_kernel,
        [sds((2, 96, 3840), BF16), sds((192, 640), BF16), sds((192, 640), BF16)],
        place,
        slopes,
        qkv_local,
        cotangent,
        w_out_local,
        positions,
        smem=(0, 1),
        scratch=[pltpu.VMEM((192, 1280), BF16)],
        flops=2 * 10**9,
        name="local",
    )
    own, one, two, three = call(
        local_weight_kernel,
        partials,
        act_own,
        swap_cores(act_other),
        flat_cot,
        swap_cores(flat_cot),
        flops=2 * 640 * 384 * 1280,
        name="local_weight",
    )
    own, one, two, three = call(
        first_sum_kernel,
        first_sums,
        own,
        along_x(one, 1),
        along_x(two, 2),
        along_x(three, 3),
        name="local_sum_x",
    )
    local_parts = [own, along_y(one, 1), along_y(two, 2), along_y(three, 3)]

    got_far = swap_cores(got.reshape(16, 96, 640)[:, 72:, :]).reshape(384, 640)
    data, cot, probs, act = call(
        group_kernel,
        [
            sds((3, 2, 192, 640), BF16),
            sds((192, 1280), BF16),
            sds((1536, 64), F32),
            sds((384, 640), BF16),
        ],
        place,
        *local_parts[1:],
        got,
        smem=(0,),
        unread=(1, 2, 3),
        scratch=[pltpu.VMEM((384, 640), BF16)],
        flops=10**11,
        name="group",
    )
    own, one, two, three, cot_far = call(
        group_weight_kernel,
        partials + [sds((192, 1280), BF16)],
        act,
        cot,
        got_far,
        flops=2 * 640 * 384 * 1280,
        name="group_weight",
    )
    a, b, c = along_y(one, 1), along_y(two, 2), along_y(three, 3)
    (back,) = call(
        group_back_kernel,
        [sds((1152, 640), BF16)],
        place,
        probs,
        data,
        cot,
        cot_far,
        w_out_global,
        smem=(0,),
        sent=True,
        scratch=[
            pltpu.VMEM((3, 2, 192, 640), BF16),
            pltpu.VMEM((2, 576, 640), BF16),
            pltpu.SemaphoreType.DMA((2,)),
        ],
        flops=2 * 10**9,
        name="group_back",
    )
    returned = exchange(back)

    own, one, two, three = call(
        first_sum_kernel,
        first_sums,
        own,
        a,
        b,
        c,
        flops=10**11,
        name="sum_y",
    )
    chunks = call(
        second_sum_kernel,
        [sds((48, 640), BF16)] * 4,
        *local_parts,
        own,
        along_x(one, 1),
        along_x(two, 2),
        along_x(three, 3),
        name="sum_x",
    )
    mine, other = call(
        unpack_kernel,
        [sds((2, 96, 1920), BF16)] * 2,
        returned,
        name="unpack",
    )
    (sums,) = call(
        sum_z_kernel,
        [sds((8, 48, 640), BF16)],
        mine,
        *[to_owner(chunk, d) for d, chunk in enumerate(chunks)],
        unread=(0,),
        name="sum_z",
    )
    pieces = lax.all_to_all(sums, "dp", split_axis=0, concat_axis=0, tiled=True)
    d_global, done = call(
        merge_kernel,
        [sds((2, 96, 3840), BF16), sds((8, 128), F32)],
        place,
        mine,
        swap_cores(other),
        smem=(0,),
        unread=(1, 2),
        sent=True,
        scratch=[pltpu.SemaphoreType.DMA((6,))],
        name="merge",
    )
    grad_local, grad_global = call(
        functools.partial(final_kernel, scale),
        [sds((40, 1280), F32), sds((40, 1280), F32)],
        done,
        pieces,
        unread=(0,),
        name="final",
    )
    return (
        d_local.reshape(1, 2, 96, 3840),
        d_global.reshape(1, 2, 96, 3840),
        grad_local,
        grad_global,
    )


def solution(mesh):
    placed = (
        P("dp", "tok", None, None),
        P("dp", "tok", None, None),
        P("dp", "tok", None),
        P(),
        P("dp", "tok", None, None),
        P(),
        P(),
    )
    return jax.shard_map(
        per_device,
        mesh=mesh,
        in_specs=placed,
        out_specs=(
            P("dp", "tok", None, None),
            P("dp", "tok", None, None),
            P("tok", None),
            P("tok", None),
        ),
        check_vma=False,
    )
```
